32 devices in a mesh: group: 2 (over y), ep: 16 (over z, x, core).
Axes of the slice: x: 2, y: 2, z: 4, core: 2. Of those that a mesh axis runs over, the one named last changes fastest.
Arguments:
- queries: bfloat16 [4096, 4096], P(('group', 'ep')), parts along dimension 0, may hold values from -8 to 8
- keys: bfloat16 [4096, 256], P(('group', 'ep')), parts along dimension 0, may hold values from -8 to 8
- values: bfloat16 [4096, 256], P(('group', 'ep')), parts along dimension 0, may hold values from -24 to 24
- segment_ids: int32 [4096], P(('group', 'ep')), parts along dimension 0, may hold values from 0 to 3, never falling along the last dimension, each value on 1 to 1024 neighbouring positions
- residual: bfloat16 [4096, 4096], P(('group', 'ep')), parts along dimension 0, may hold values from -6 to 6
- norm_gain: bfloat16 [4096], replicated, may hold values from 0.5 to 1.5
- route_ids: int32 [4096, 2], P(('group', 'ep')), parts along dimension 0, may hold values from 0 to 7, all different within a row; in each aligned block of 128 rows (0 to 127, 128 to 255, ...) at most 64 rows name the same one
- route_weights: float32 [4096, 2], P(('group', 'ep')), parts along dimension 0, may hold values from 0.2 to 1
- w_gate: bfloat16 [16, 4096, 384], P('ep'), may hold values from -0.09375 to 0.09375
- w_up: bfloat16 [16, 4096, 384], P('ep'), may hold values from -0.09375 to 0.09375
- w_down: bfloat16 [16, 384, 4096], P('ep'), may hold values from -0.21875 to 0.21875
Outputs:
- layer_out: bfloat16 [4096, 4096], P(('group', 'ep')), parts along dimension 0
The draws below stay inside these ranges and needn't reach their ends.
There are 2 independent parts, one for each index of `group`. The reference program is written for one: setup_inputs(seed, part) draws one part's arguments, and reference() takes and returns one part's arrays. A program takes and returns all parts, laid end to end along the dimension named above; an argument that names none is the same for every part. Nothing has to cross between parts.
Inputs may be any that keep to these rules, and one draw needn't show every extreme that they name: `segment_ids`: document ids never fall along the row; a document holds 1 to 1024 tokens. `route_ids`: each token names 2 different experts; among the 128 tokens of one device no expert is named more than 64 times.
All inputs are finite; a program needn't handle non-finite values.
Results may differ from the reference program's by a relative error of at most 0.007.
Values may be sent and summed in bfloat16 or wider, within the bound.
A program may use at most 128 MiB of HBM per device.

```python
import math
import jax
import jax.numpy as jnp
import numpy as np
from jax import lax

D = 4096
HEAD_SIZE = 128
QUERY_HEADS = 32
KEY_VALUE_HEADS = 2
FFE = 768
TOPK = 2
REACH = 8
TOKENS_PER_SHARD = 128
EXPERTS = 8
PACKED_TOKENS = 2048
MOST = 1024
DOCS = 4
CAP = 64
N_EP = 16


def draw_queries(key, part):
    key = jax.random.fold_in(key, 5)
    base_offset = jax.random.normal(key, (PACKED_TOKENS, KEY_VALUE_HEADS, QUERY_HEADS // KEY_VALUE_HEADS, HEAD_SIZE), jnp.float32)
    return jnp.clip(base_offset, -8.0, 8.0).reshape(PACKED_TOKENS, QUERY_HEADS * HEAD_SIZE).astype(jnp.bfloat16)


def draw_keys(key, part):
    key = jax.random.fold_in(key, 9)
    base_offset = jax.random.normal(key, (PACKED_TOKENS, KEY_VALUE_HEADS, HEAD_SIZE), jnp.float32)
    return jnp.clip(base_offset, -8.0, 8.0).reshape(PACKED_TOKENS, KEY_VALUE_HEADS * HEAD_SIZE).astype(jnp.bfloat16)


def shard_levels(stream_key, shape, cuts, smallest, high):
    level = 1.0
    for dim, shards_of in cuts:
        heights = jax.random.uniform(jax.random.fold_in(jax.random.fold_in(stream_key, 6), dim), (shards_of,), jnp.float32, smallest / len(cuts), high / len(cuts))
        level = level * jnp.repeat(jnp.exp(heights), shape[dim] // shards_of).reshape((-1,) + (1,) * (len(shape) - 1 - dim))
    return level


def split_up(number_of, total, bound, skew):
    weights = [(1 << 20) // math.isqrt(standing ** skew) + 1 for standing in range(2, number_of + 1)]
    rest, holding = total - bound - (number_of - 1), [1] * (number_of - 1)
    while rest > 0:
        movable = [i for i in range(number_of - 1) if holding[i] < bound]
        pool, left = sum([weights[i] for i in movable]), rest
        for i in movable:
            more = min(bound - holding[i], max(1, left * weights[i] // pool), rest)
            holding[i] = holding[i] + more
            rest = rest - more
    return np.array([bound] + holding)


def ragged(stream_key, amount, total, limit, lean):
    if amount == 2:
        one = jax.random.randint(stream_key, (), max(1, total - limit), min(limit, total - 1) + 1)
        return jnp.stack([one, total - one])
    lengths = jnp.asarray(split_up(amount, total, limit, lean), jnp.int32)
    twos = (amount - 1) // 2
    giver, sink = lengths[1:1 + 2 * twos:2], lengths[2:2 + 2 * twos:2]
    margin = jnp.minimum(giver - 1, limit - sink)
    shifted = jax.random.randint(jax.random.fold_in(stream_key, 1), (twos,), 0, 1 << 20) % (margin + 1)
    lengths = lengths.at[1:1 + 2 * twos:2].set(giver - shifted).at[2:2 + 2 * twos:2].set(sink + shifted)
    return lengths[jax.random.permutation(jax.random.fold_in(stream_key, 2), amount)]


def assign_block(own_key, own, number, rows, amount, top, bound, lean):
    sequence = jax.random.permutation(own_key, amount)
    crowded, ordinary = portions_of(amount, rows * top, bound, lean, True), portions_of(amount, rows * top, bound, lean, False)
    places = jnp.arange(amount)

    def named(tallies, rotation):
        used = int((tallies > 0).sum())
        fixed = max(1, used // 4)
        shifted = fixed + (places - fixed + rotation * (used - fixed)) % max(1, amount - fixed)
        return jnp.zeros((amount,), jnp.int32).at[sequence[jnp.where(places < fixed, places, shifted)]].set(jnp.asarray(tallies, jnp.int32))

    tallies = jnp.where(number % 4 == 0, named(crowded, number // 4), named(ordinary, number - number // 4 - 1))
    mixed = jax.random.permutation(jax.random.fold_in(own, 3), amount)
    giver, sink = mixed[0:amount // 2 * 2:2], mixed[1:amount // 2 * 2:2]
    slack = jnp.minimum(tallies[giver] - 1, bound - tallies[sink]) // 2
    slack = jnp.where((giver == sequence[0]) | (sink == sequence[0]) | (tallies[sink] == 0), 0, jnp.maximum(slack, 0))
    shifted = jax.random.randint(jax.random.fold_in(own, 4), (amount // 2,), 0, 1 << 20) % (slack + 1)
    tallies = tallies.at[giver].add(-shifted).at[sink].add(shifted)
    labels = jnp.searchsorted(jnp.cumsum(tallies), jnp.arange(rows * top), side="right").astype(jnp.int32)
    listing = labels.reshape(top, rows).T
    listing = listing[jax.random.permutation(jax.random.fold_in(own, 1), rows)]
    rotation = jax.random.randint(jax.random.fold_in(own, 2), (rows, 1), 0, top)
    return jnp.take_along_axis(listing, (jnp.arange(top)[None, :] + rotation) % top, axis=1)


def portions_of(number_of, total, reach, slope, full):
    loads = [(1 << 20) // math.isqrt(grade ** slope) + 1 for grade in range(1, number_of + 1)]
    largest = reach if full else min(reach, max(-(-total // number_of), total * loads[0] // sum(loads)))
    least = 1 if total - largest >= number_of - 1 else 0
    holding, surplus = [largest] + [least] * (number_of - 1), total - largest - least * (number_of - 1)
    while surplus > 0:
        candidates = [i for i in range(1, number_of) if holding[i] < largest] or [i for i in range(1, number_of) if holding[i] < reach]
        mass, left = sum([loads[i] for i in candidates]), surplus
        for i in candidates:
            extra = min(reach - holding[i], max(1, left * loads[i] // mass), surplus)
            holding[i] = holding[i] + extra
            surplus = surplus - extra
    return np.array(holding)


def normal_values(key, dims, spread, limit, shards=(), kind=jnp.bfloat16):
    result = jax.random.normal(key, dims, jnp.float32) * spread
    if len(shards) > 0:
        result = shard_levels(key, dims, shards, -0.22, 0.18) * result
    return jnp.clip(result, min=-limit, max=limit).astype(kind)


def setup_inputs(seed: int = 0, part: int = 0) -> dict:
    key_list = jax.random.split(jax.random.key(seed), 12)
    part_splits = jax.random.split(jax.random.fold_in(key_list[11], part), 12)
    queries = draw_queries(jax.random.fold_in(jax.random.fold_in(key_list[11], part), 71), part)
    keys = draw_keys(jax.random.fold_in(jax.random.fold_in(key_list[11], part), 71), part)
    values = normal_values(part_splits[2], (PACKED_TOKENS, KEY_VALUE_HEADS * HEAD_SIZE), 4.0, 24.0, ((0, 16),))
    segment_ids = jnp.searchsorted(jnp.cumsum(ragged(part_splits[3], DOCS, PACKED_TOKENS, MOST, 2)), jnp.arange(PACKED_TOKENS), side="right").astype(jnp.int32)
    residual = normal_values(part_splits[4], (PACKED_TOKENS, D), 1.0, 6.0, ((0, 16),))
    norm_gain = jnp.clip(1.0 + 0.1 * jax.random.normal(key_list[5], (D,), jnp.float32), 0.5, 1.5).astype(jnp.bfloat16)
    route_ids_keys = jax.random.split(jax.random.fold_in(part_splits[6], 1), PACKED_TOKENS // TOKENS_PER_SHARD)
    route_ids_turns = jax.random.permutation(jax.random.fold_in(part_splits[6], 3), PACKED_TOKENS // TOKENS_PER_SHARD)
    route_ids = jax.vmap(lambda own, number: assign_block(jax.random.fold_in(part_splits[6], 2), own, number, TOKENS_PER_SHARD, EXPERTS, TOPK, CAP, 2))(route_ids_keys, route_ids_turns).reshape((PACKED_TOKENS, TOPK))
    route_weights = jnp.clip(0.2 + 0.8 * jax.random.uniform(part_splits[7], (PACKED_TOKENS, TOPK), jnp.float32) ** shard_levels(part_splits[7], (PACKED_TOKENS, TOPK), ((0, 16),), -0.2, 0.2), 0.2, 1.0)
    w_gate = normal_values(key_list[8], (2 * EXPERTS, D, FFE // 2), D ** -0.5, 0.09375, ((0, 16),))
    w_up = normal_values(key_list[9], (2 * EXPERTS, D, FFE // 2), D ** -0.5, 0.09375, ((0, 16),))
    w_down = normal_values(key_list[10], (2 * EXPERTS, FFE // 2, D), FFE ** -0.5, 0.21875, ((0, 16),))
    return dict(queries=queries, keys=keys, values=values, segment_ids=segment_ids, residual=residual, norm_gain=norm_gain, route_ids=route_ids, route_weights=route_weights, w_gate=w_gate, w_up=w_up, w_down=w_down)


NEGATIVE = -1e+30

def expert_half(rows, gate_half, up_half, down_half):
    gate = jnp.dot(rows, gate_half, preferred_element_type=jnp.float32)
    upward = jnp.dot(rows, up_half, preferred_element_type=jnp.float32)
    hidden = (jax.nn.silu(gate) * upward).astype(jnp.bfloat16)
    return jnp.dot(hidden, down_half, preferred_element_type=jnp.float32).astype(jnp.bfloat16)

def reference(queries, keys, values, segment_ids, residual, norm_gain, route_ids, route_weights, w_gate, w_up, w_down):
    query_head_group = QUERY_HEADS // KEY_VALUE_HEADS
    window_span = (REACH + 1) * TOKENS_PER_SHARD
    border_margin = REACH * TOKENS_PER_SHARD
    key_padding = jnp.concatenate([jnp.zeros((border_margin, KEY_VALUE_HEADS * HEAD_SIZE), keys.dtype), keys], 0)
    value_padding = jnp.concatenate([jnp.zeros((border_margin, KEY_VALUE_HEADS * HEAD_SIZE), values.dtype), values], 0)
    seg_pad = jnp.concatenate([jnp.full((border_margin,), -1, jnp.int32), segment_ids.astype(jnp.int32)], 0)
    scale = 1.0 / HEAD_SIZE ** 0.5

    def block(index):
        start_index = (index * TOKENS_PER_SHARD).astype(jnp.int32)
        query_tiles = lax.dynamic_slice_in_dim(queries, start_index, TOKENS_PER_SHARD, 0).reshape(TOKENS_PER_SHARD, KEY_VALUE_HEADS, query_head_group, HEAD_SIZE).astype(jnp.float32)
        key_tiles = lax.dynamic_slice_in_dim(key_padding, start_index, window_span, 0).reshape(window_span, KEY_VALUE_HEADS, HEAD_SIZE).astype(jnp.float32)
        value_tiles = lax.dynamic_slice_in_dim(value_padding, start_index, window_span, 0).reshape(window_span, KEY_VALUE_HEADS, HEAD_SIZE).astype(jnp.float32)
        query_seg = lax.dynamic_slice_in_dim(segment_ids.astype(jnp.int32), start_index, TOKENS_PER_SHARD, 0)
        key_seg = lax.dynamic_slice_in_dim(seg_pad, start_index, window_span, 0)
        query_pos = start_index + jnp.arange(TOKENS_PER_SHARD, dtype=jnp.int32)
        key_pos = start_index - border_margin + jnp.arange(window_span, dtype=jnp.int32)
        allowed = (key_seg[None, :] == query_seg[:, None]) & (key_pos[None, :] <= query_pos[:, None]) & (key_pos[None, :] >= 0)
        scores = jnp.einsum('tgjd,sgd->tgjs', query_tiles, key_tiles) * scale
        scores = jnp.where(allowed[:, None, None, :], scores, NEGATIVE)
        highest = lax.optimization_barrier(jnp.max(scores, -1, keepdims=True))
        expo = jnp.exp(scores - highest)
        probs = lax.optimization_barrier(expo.astype(jnp.bfloat16)).astype(jnp.float32)
        total = lax.optimization_barrier(jnp.sum(expo, -1))
        summed = jnp.einsum('tgjs,sgd->tgjd', probs, value_tiles)
        return (summed / total[..., None]).reshape(TOKENS_PER_SHARD, QUERY_HEADS * HEAD_SIZE).astype(jnp.bfloat16)
    attended = lax.map(block, jnp.arange(N_EP, dtype=jnp.int32)).reshape(PACKED_TOKENS, D)
    stream = (residual.astype(jnp.float32) + attended.astype(jnp.float32)).astype(jnp.bfloat16)
    stream_f = stream.astype(jnp.float32)
    normed = (stream_f * lax.rsqrt(lax.optimization_barrier(jnp.mean(stream_f * stream_f, -1, keepdims=True)) + 1e-06) * norm_gain.astype(jnp.float32)).astype(jnp.bfloat16)
    pairs = PACKED_TOKENS * TOPK
    flat = route_ids.reshape(-1).astype(jnp.int32)
    order = jnp.argsort(flat, stable=True).astype(jnp.int32)
    counts = jnp.zeros((EXPERTS,), jnp.int32).at[flat].add(1)
    starts = (jnp.cumsum(counts) - counts).astype(jnp.int32)
    rows_max = N_EP * CAP
    order_pad = jnp.concatenate([order, jnp.full((rows_max,), pairs, jnp.int32)])
    normed_pad = jnp.concatenate([normed, jnp.zeros((1, D), jnp.bfloat16)], 0)

    def one_expert(expert, gathered):
        expert = jnp.asarray(expert).astype(jnp.int32)
        index_list = lax.dynamic_slice_in_dim(order_pad, starts[expert], rows_max, 0)
        valid = jnp.arange(rows_max, dtype=jnp.int32) < counts[expert]
        index_list = jnp.where(valid, index_list, pairs).astype(jnp.int32)
        rows = normed_pad[index_list // TOPK]
        first = expert_half(rows, w_gate[2 * expert], w_up[2 * expert], w_down[2 * expert])
        second = expert_half(rows, w_gate[2 * expert + 1], w_up[2 * expert + 1], w_down[2 * expert + 1])
        output = (first.astype(jnp.float32) + second.astype(jnp.float32)).astype(jnp.bfloat16)
        return gathered.at[index_list].set(output, mode='drop')
    gathered = lax.fori_loop(0, EXPERTS, one_expert, jnp.zeros((pairs, D), jnp.bfloat16))
    mixed = lax.optimization_barrier(jnp.sum(route_weights.astype(jnp.float32)[:, :, None] * gathered.reshape(PACKED_TOKENS, TOPK, D).astype(jnp.float32), 1))
    return (stream_f + mixed).astype(jnp.bfloat16)
```

```python
import functools
import math

import jax
import jax.numpy as jnp
from jax import lax
from jax.experimental import pallas as pl
from jax.experimental.pallas import tpu as pltpu
from jax.sharding import PartitionSpec as P

HEAD_SIZE = 128
REACH = 8
NEGATIVE = -1e30
MESH = pl.DeviceIdType.MESH
SEG_ROWS = 16


def nt_dot(a, b):
    return lax.dot_general(a, b, (((1,), (1,)), ((), ())), preferred_element_type=jnp.float32)


def attention_kernel(
    n, kv_heads, q_ref, kv_ref, segcol_ref, res_ref, gain_ref, place_ref,
    stream_ref, rows_ref,
    held, bias, attended, normed, send_sem, recv_sem,
):
    me = lax.axis_index("ep")
    rows = q_ref.shape[0]
    heads = q_ref.shape[1] // HEAD_SIZE
    per_kv = heads // kv_heads
    kv_width = kv_heads * HEAD_SIZE
    span = rows + SEG_ROWS
    reach = min(REACH, n - 1)

    barrier = pltpu.get_barrier_semaphore()
    for d in range(1, reach + 1):
        pl.semaphore_signal(
            barrier, inc=1, device_id={"ep": lax.rem(me + n - d, n)}, device_id_type=MESH
        )
    pl.semaphore_wait(barrier, reach)

    copies = []
    for d in range(1, reach + 1):
        copy = pltpu.make_async_remote_copy(
            src_ref=kv_ref, dst_ref=held.at[d],
            send_sem=send_sem.at[d], recv_sem=recv_sem.at[d],
            device_id={"ep": lax.rem(me + d, n)}, device_id_type=MESH,
        )
        copy.start()
        copies.append(copy)
    held[0] = kv_ref[...]
    for copy in copies:
        copy.wait()

    query_seg = segcol_ref[...]
    t = lax.broadcasted_iota(jnp.int32, (rows, rows), 0)
    u = lax.broadcasted_iota(jnp.int32, (rows, rows), 1)
    for d in range(reach + 1):
        key_seg = held[d, rows : rows + SEG_ROWS, 0:rows][0:1].astype(jnp.float32)
        allowed = (key_seg == query_seg) & (u - d * rows <= t) & (u + (me - d) * rows >= 0)
        bias[:, d * rows : (d + 1) * rows] = jnp.where(allowed, 0.0, NEGATIVE)

    scale = math.log2(math.e) / math.sqrt(HEAD_SIZE)

    def one_head(h, g):
        col = pl.multiple_of(h * HEAD_SIZE, HEAD_SIZE)
        q = q_ref[:, pl.ds(col, HEAD_SIZE)]
        k = jnp.concatenate(
            [held[d, 0:rows, g * HEAD_SIZE : (g + 1) * HEAD_SIZE] for d in range(reach + 1)], 0
        )
        v = jnp.concatenate(
            [
                held[d, 0:rows, kv_width + g * HEAD_SIZE : kv_width + (g + 1) * HEAD_SIZE]
                for d in range(reach + 1)
            ],
            0,
        )
        s = nt_dot(q, k) * scale + bias[...]
        top = jnp.max(s, -1, keepdims=True)
        p = jnp.exp2(s - top)
        total = jnp.sum(p, -1, keepdims=True)
        pv = jnp.dot(p.astype(jnp.bfloat16), v, preferred_element_type=jnp.float32)
        attended[:, pl.ds(col, HEAD_SIZE)] = (pv / total).astype(jnp.bfloat16)

    def heads_step(i, carry):
        for g in range(kv_heads):
            one_head(i + g * per_kv, g)
        return carry

    lax.fori_loop(0, per_kv, heads_step, 0)

    chunk = 16

    def norm_step(i, carry):
        r = pl.ds(pl.multiple_of(i * chunk, chunk), chunk)
        stream = (res_ref[r, :].astype(jnp.float32) + attended[r, :].astype(jnp.float32)).astype(
            jnp.bfloat16
        )
        stream_ref[r, :] = stream
        sf = stream.astype(jnp.float32)
        inv = lax.rsqrt(jnp.mean(sf * sf, -1, keepdims=True) + 1e-06)
        normed[r, :] = (sf * inv * gain_ref[...].astype(jnp.float32)).astype(jnp.bfloat16)
        return carry

    lax.fori_loop(0, rows // chunk, norm_step, 0)

    tile = 512

    def place_step(i, carry):
        c = pl.ds(pl.multiple_of(i * tile, tile), tile)
        rows_ref[:, c] = jnp.dot(
            place_ref[...], normed[:, c], preferred_element_type=jnp.float32
        ).astype(jnp.bfloat16)
        return carry

    lax.fori_loop(0, normed.shape[1] // tile, place_step, 0)


def attention(n, kv_heads, queries, kv, segcol, residual, gain, place):
    rows, width = queries.shape
    reach = min(REACH, n - 1)
    vmem = pl.BlockSpec(memory_space=pltpu.VMEM)
    return pl.pallas_call(
        functools.partial(attention_kernel, n, kv_heads),
        out_shape=(
            jax.ShapeDtypeStruct((rows, width), jnp.bfloat16),
            jax.ShapeDtypeStruct((place.shape[0], width), jnp.bfloat16),
        ),
        in_specs=[vmem] * 6,
        out_specs=(vmem, vmem),
        scratch_shapes=[
            pltpu.VMEM((reach + 1,) + kv.shape, jnp.bfloat16),
            pltpu.VMEM((rows, (reach + 1) * rows), jnp.float32),
            pltpu.VMEM((rows, width), jnp.bfloat16),
            pltpu.VMEM((rows, width), jnp.bfloat16),
            pltpu.SemaphoreType.DMA((reach + 1,)),
            pltpu.SemaphoreType.DMA((reach + 1,)),
        ],
        compiler_params=pltpu.CompilerParams(
            collective_id=0, has_side_effects=True, vmem_limit_bytes=40 * 1024 * 1024
        ),
        name="attention",
    )(queries, kv, segcol, residual, gain, place)


def local(
    queries, keys, values, segment_ids, residual, norm_gain, route_ids, route_weights,
    w_gate, w_up, w_down,
):
    rows, width = residual.shape
    n = lax.axis_size("ep")
    kv_heads = keys.shape[1] // HEAD_SIZE
    n_experts = n // 2
    topk = route_ids.shape[1]
    capacity = max(2, 2 * rows * topk // n_experts)

    swap = [(i, i ^ 1) for i in range(n)]
    core = lax.rem(lax.axis_index("ep"), 2)
    other_gate = lax.ppermute(w_gate[0], "ep", swap)
    other_up = lax.ppermute(w_up[0], "ep", swap)
    other_down = lax.ppermute(w_down[0], "ep", swap)

    seg_row = jnp.zeros((SEG_ROWS, 2 * keys.shape[1]), jnp.bfloat16)
    seg_row = lax.dynamic_update_slice(
        seg_row, jnp.broadcast_to(segment_ids.astype(jnp.bfloat16)[None, :], (SEG_ROWS, rows)), (0, 0)
    )
    kv = jnp.concatenate([jnp.concatenate([keys, values], 1), seg_row], 0)
    segcol = segment_ids.astype(jnp.float32)[:, None]

    experts = jnp.arange(n_experts, dtype=jnp.int32)
    hit = route_ids[:, :, None] == experts[None, None, :]
    named = jnp.any(hit, 1)
    weight = jnp.sum(jnp.where(hit, route_weights[:, :, None], 0.0), 1)
    below = jnp.tril(jnp.ones((rows, rows), jnp.bfloat16), -1)
    slot = jnp.dot(below, named.astype(jnp.bfloat16), preferred_element_type=jnp.float32).astype(jnp.int32)
    code = jnp.where(named, slot, -1)
    slots = jnp.arange(capacity, dtype=jnp.int32)
    place = (code.T[:, None, :] == slots[None, :, None]).astype(jnp.bfloat16)
    place = place.reshape(n_experts * capacity, rows)
    mix = jnp.where(code[:, :, None] == slots[None, None, :], weight[:, :, None], 0.0)
    mix = mix.reshape(rows, n_experts * capacity)
    mix_hi = mix.astype(jnp.bfloat16)
    mix_lo = (mix - mix_hi.astype(jnp.float32)).astype(jnp.bfloat16)

    stream, outgoing = attention(n, kv_heads, queries, kv, segcol, residual, norm_gain[None, :], place)

    groups = [[c for c in range(k, n, 2)] for k in range(2)]
    arrived = lax.all_to_all(
        outgoing.reshape(n_experts, capacity, width), "ep", split_axis=0, concat_axis=0,
        axis_index_groups=groups, tiled=True,
    ).reshape(-1, width)

    def half(gate_half, up_half, down_half):
        gate = jnp.dot(arrived, gate_half, preferred_element_type=jnp.float32)
        upward = jnp.dot(arrived, up_half, preferred_element_type=jnp.float32)
        hidden = (jax.nn.silu(gate) * upward).astype(jnp.bfloat16)
        return jnp.dot(hidden, down_half, preferred_element_type=jnp.float32)

    out = half(w_gate[0], w_up[0], w_down[0]) + half(other_gate, other_up, other_down)
    returned = lax.all_to_all(
        out.astype(jnp.bfloat16).reshape(n_experts, capacity, width), "ep", split_axis=0,
        concat_axis=0, axis_index_groups=groups, tiled=True,
    ).reshape(-1, width)
    mixed = jnp.dot(mix_hi, returned, preferred_element_type=jnp.float32) + jnp.dot(
        mix_lo, returned, preferred_element_type=jnp.float32
    )
    return (stream.astype(jnp.float32) + mixed).astype(jnp.bfloat16)


def solution(mesh):
    tokens = P(("group", "ep"), None)
    split = P("ep", None, None)
    placed = (
        tokens, tokens, tokens, P(("group", "ep")), tokens, P(), tokens, tokens, split, split, split,
    )
    return jax.shard_map(local, mesh=mesh, in_specs=placed, out_specs=tokens, check_vma=False)
```

```python
import functools
import math

import jax
import jax.numpy as jnp
from jax import lax
from jax.experimental import pallas as pl
from jax.experimental.pallas import tpu as pltpu
from jax.sharding import PartitionSpec as P

HEAD_SIZE = 128
REACH = 8
NEGATIVE = -1e30
MESH = pl.DeviceIdType.MESH
SEG_ROWS = 16


def nt_dot(a, b):
    return lax.dot_general(a, b, (((1,), (1,)), ((), ())), preferred_element_type=jnp.float32)


def attention_kernel(
    n, kv_heads, placing, q_ref, kv_ref, segcol_ref, res_ref, gain_ref, *rest
):
    if placing:
        place_ref, stream_ref, rows_ref, held, bias, attended, normed, send_sem, recv_sem = rest
    else:
        stream_ref, normed, held, bias, attended, send_sem, recv_sem = rest
    me = lax.axis_index("ep")
    rows = q_ref.shape[0]
    heads = q_ref.shape[1] // HEAD_SIZE
    per_kv = heads // kv_heads
    kv_width = kv_heads * HEAD_SIZE
    span = rows + SEG_ROWS
    reach = min(REACH, n - 1)

    barrier = pltpu.get_barrier_semaphore()
    for d in range(1, reach + 1):
        pl.semaphore_signal(
            barrier, inc=1, device_id={"ep": lax.rem(me + n - d, n)}, device_id_type=MESH
        )
    pl.semaphore_wait(barrier, reach)

    copies = []
    for d in range(1, reach + 1):
        copy = pltpu.make_async_remote_copy(
            src_ref=kv_ref, dst_ref=held.at[d],
            send_sem=send_sem.at[d], recv_sem=recv_sem.at[d],
            device_id={"ep": lax.rem(me + d, n)}, device_id_type=MESH,
        )
        copy.start()
        copies.append(copy)
    held[0] = kv_ref[...]
    for copy in copies:
        copy.wait()

    query_seg = segcol_ref[...]
    t = lax.broadcasted_iota(jnp.int32, (rows, rows), 0)
    u = lax.broadcasted_iota(jnp.int32, (rows, rows), 1)
    for d in range(reach + 1):
        key_seg = held[d, rows : rows + SEG_ROWS, 0:rows][0:1].astype(jnp.float32)
        allowed = (key_seg == query_seg) & (u - d * rows <= t) & (u + (me - d) * rows >= 0)
        bias[:, d * rows : (d + 1) * rows] = jnp.where(allowed, 0.0, NEGATIVE)

    scale = math.log2(math.e) / math.sqrt(HEAD_SIZE)

    def one_head(h, g):
        col = pl.multiple_of(h * HEAD_SIZE, HEAD_SIZE)
        q = q_ref[:, pl.ds(col, HEAD_SIZE)]
        k = jnp.concatenate(
            [held[d, 0:rows, g * HEAD_SIZE : (g + 1) * HEAD_SIZE] for d in range(reach + 1)], 0
        )
        v = jnp.concatenate(
            [
                held[d, 0:rows, kv_width + g * HEAD_SIZE : kv_width + (g + 1) * HEAD_SIZE]
                for d in range(reach + 1)
            ],
            0,
        )
        s = nt_dot(q, k) * scale + bias[...]
        top = jnp.max(s, -1, keepdims=True)
        p = jnp.exp2(s - top)
        total = jnp.sum(p, -1, keepdims=True)
        pv = jnp.dot(p.astype(jnp.bfloat16), v, preferred_element_type=jnp.float32)
        attended[:, pl.ds(col, HEAD_SIZE)] = (pv / total).astype(jnp.bfloat16)

    def heads_step(i, carry):
        for g in range(kv_heads):
            one_head(i + g * per_kv, g)
        return carry

    lax.fori_loop(0, per_kv, heads_step, 0)

    chunk = 16

    def norm_step(i, carry):
        r = pl.ds(pl.multiple_of(i * chunk, chunk), chunk)
        stream = (res_ref[r, :].astype(jnp.float32) + attended[r, :].astype(jnp.float32)).astype(
            jnp.bfloat16
        )
        stream_ref[r, :] = stream
        sf = stream.astype(jnp.float32)
        inv = lax.rsqrt(jnp.mean(sf * sf, -1, keepdims=True) + 1e-06)
        normed[r, :] = (sf * inv * gain_ref[...].astype(jnp.float32)).astype(jnp.bfloat16)
        return carry

    lax.fori_loop(0, rows // chunk, norm_step, 0)

    if not placing:
        return
    tile = 512

    def place_step(i, carry):
        c = pl.ds(pl.multiple_of(i * tile, tile), tile)
        rows_ref[:, c] = jnp.dot(
            place_ref[...], normed[:, c], preferred_element_type=jnp.float32
        ).astype(jnp.bfloat16)
        return carry

    lax.fori_loop(0, normed.shape[1] // tile, place_step, 0)


def attention(n, kv_heads, queries, kv, segcol, residual, gain, place=None):
    rows, width = queries.shape
    reach = min(REACH, n - 1)
    vmem = pl.BlockSpec(memory_space=pltpu.VMEM)
    placing = place is not None
    sent = place.shape[0] if placing else rows
    operands = (queries, kv, segcol, residual, gain) + ((place,) if placing else ())
    scratch = [
        pltpu.VMEM((reach + 1,) + kv.shape, jnp.bfloat16),
        pltpu.VMEM((rows, (reach + 1) * rows), jnp.float32),
        pltpu.VMEM((rows, width), jnp.bfloat16),
    ]
    if placing:
        scratch.append(pltpu.VMEM((rows, width), jnp.bfloat16))
    return pl.pallas_call(
        functools.partial(attention_kernel, n, kv_heads, placing),
        out_shape=(
            jax.ShapeDtypeStruct((rows, width), jnp.bfloat16),
            jax.ShapeDtypeStruct((sent, width), jnp.bfloat16),
        ),
        in_specs=[vmem] * len(operands),
        out_specs=(vmem, vmem),
        scratch_shapes=scratch + [
            pltpu.SemaphoreType.DMA((reach + 1,)),
            pltpu.SemaphoreType.DMA((reach + 1,)),
        ],
        compiler_params=pltpu.CompilerParams(
            collective_id=0, has_side_effects=True, vmem_limit_bytes=40 * 1024 * 1024
        ),
        name="attention",
    )(*operands)


def experts_kernel(
    n, capacity, tokens_ref, stream_ref, codes_ref, hi_ref, lo_ref,
    gate0, up0, down0, gate1, up1, down1,
    out_ref,
    line, x_out, x_in, feed, hidden, result, returned, w_gate, w_up, w_down,
    w_sem, recv_sem, up_sem, down_sem, x_send, x_recv, back_send, back_recv,
):
    planes = n // 4
    n_experts = n // 2
    last = planes - 1
    me = lax.axis_index("ep")
    z = me // 4
    x = lax.rem(me // 2, 2)
    c = lax.rem(me, 2)
    expert = me // 2
    partner = me + 2 - 4 * x
    partner_expert = expert + 1 - 2 * x
    rows, width = tokens_ref.shape
    ffe = down0.shape[0]

    barrier = pltpu.get_barrier_semaphore()
    for k in range(1, n_experts):
        pl.semaphore_signal(
            barrier, inc=1, device_id={"ep": lax.rem(me + 2 * k, n)}, device_id_type=MESH
        )

    loads = []
    for j, (g, u, d) in enumerate(((gate0, up0, down0), (gate1, up1, down1))):
        part = pl.ds(j * ffe, ffe)
        for k, (src, dst) in enumerate(
            ((g, w_gate.at[:, part]), (u, w_up.at[:, part]), (d, w_down.at[part, :]))
        ):
            load = pltpu.make_async_copy(src, dst, w_sem.at[3 * j + k])
            load.start()
            loads.append(load)

    line[z] = tokens_ref[...]
    pl.semaphore_wait(barrier, n_experts - 1)

    def hop(b, upward):
        return pltpu.make_async_remote_copy(
            src_ref=line.at[b], dst_ref=line.at[b],
            send_sem=(up_sem if upward else down_sem).at[b], recv_sem=recv_sem.at[b],
            device_id={"ep": lax.rem(me + 4, n) if upward else lax.rem(me + n - 4, n)},
            device_id_type=MESH,
        )

    def swap(b):
        return pltpu.make_async_remote_copy(
            src_ref=x_out.at[b], dst_ref=x_in.at[b],
            send_sem=x_send.at[b], recv_sem=x_recv.at[b],
            device_id={"ep": partner}, device_id_type=MESH,
        )

    def back(b, other):
        side = 1 - x if other else x
        return pltpu.make_async_remote_copy(
            src_ref=result.at[b, pl.ds(capacity * other, capacity)],
            dst_ref=returned.at[pl.ds(pl.multiple_of(expert * capacity, capacity), capacity)],
            send_sem=back_send.at[2 * b + other], recv_sem=back_recv.at[expert],
            device_id={"ep": b * 4 + side * 2 + c}, device_id_type=MESH,
        )

    slots = lax.broadcasted_iota(jnp.int32, (capacity, rows), 0).astype(jnp.float32)
    tile = 512
    tiles = width // tile

    def pack(b, e, put):
        source = b * 4 + x * 2 + c
        place = (codes_ref[source * n_experts + e] == slots).astype(jnp.bfloat16)

        def step(i, carry):
            col = pl.ds(pl.multiple_of(i * tile, tile), tile)
            put(col, jnp.dot(
                place, line[b, :, col], preferred_element_type=jnp.float32
            ).astype(jnp.bfloat16))
            return carry

        lax.fori_loop(0, tiles, step, 0)

    def arrive(b):
        @pl.when(b != z)
        def _():
            hop(b, True).wait_recv()

        @pl.when((b <= z) & (z < last))
        def _():
            hop(b, True).start()

        @pl.when((b >= z) & (z > 0))
        def _():
            hop(b, False).start()

        def put(col, value):
            x_out[b, :, col] = value

        pack(b, partner_expert, put)
        swap(b).start()

    def order(i):
        low = jnp.minimum(z, last - z)
        b = jnp.where((low == 1) & (i < 2), 1 - i, i)
        return jnp.where(z < planes // 2, b, last - b)

    def put_feed(col, value):
        feed[0:capacity, col] = value

    hidden_tile = 256

    def step(i, carry):
        b = order(i)
        inner = (z > 0) & (z < last)

        @pl.when((i != 2) | jnp.logical_not(inner))
        def _():
            arrive(b)

        @pl.when((i == 1) & inner)
        def _():
            arrive(order(2))

        pack(b, expert, put_feed)

        @pl.when(i == 0)
        def _():
            for load in loads:
                load.wait()

        swap(b).wait_recv()
        feed[capacity : 2 * capacity, :] = x_in[b]

        def hidden_step(k, inner_carry):
            col = pl.ds(pl.multiple_of(k * hidden_tile, hidden_tile), hidden_tile)
            gate = jnp.dot(feed[...], w_gate[:, col], preferred_element_type=jnp.float32)
            upward = jnp.dot(feed[...], w_up[:, col], preferred_element_type=jnp.float32)
            hidden[:, col] = (jax.nn.silu(gate) * upward).astype(jnp.bfloat16)
            return inner_carry

        lax.fori_loop(0, 2 * ffe // hidden_tile, hidden_step, 0)

        def down_step(k, inner_carry):
            col = pl.ds(pl.multiple_of(k * tile, tile), tile)
            result[b, :, col] = jnp.dot(
                hidden[...], w_down[:, col], preferred_element_type=jnp.float32
            ).astype(jnp.bfloat16)
            return inner_carry

        lax.fori_loop(0, tiles, down_step, 0)

        back(b, 1).start()

        @pl.when(b != z)
        def _():
            back(b, 0).start()

        @pl.when(b == z)
        def _():
            returned[pl.ds(pl.multiple_of(expert * capacity, capacity), capacity), :] = result[
                b, 0:capacity
            ]

        return carry

    lax.fori_loop(0, planes, step, 0)

    for e in range(n_experts):
        @pl.when(expert != e)
        def _():
            pltpu.make_async_remote_copy(
                src_ref=result.at[0, pl.ds(0, capacity)],
                dst_ref=returned.at[pl.ds(e * capacity, capacity)],
                send_sem=back_send.at[0], recv_sem=back_recv.at[e],
                device_id={"ep": partner}, device_id_type=MESH,
            ).wait_recv()

    def mix_step(i, carry):
        col = pl.ds(pl.multiple_of(i * tile, tile), tile)
        picked = returned[:, col]
        mixed = jnp.dot(hi_ref[...], picked, preferred_element_type=jnp.float32)
        mixed += jnp.dot(lo_ref[...], picked, preferred_element_type=jnp.float32)
        out_ref[:, col] = (stream_ref[:, col].astype(jnp.float32) + mixed).astype(jnp.bfloat16)
        return carry

    lax.fori_loop(0, tiles, mix_step, 0)

    for b in range(planes):
        @pl.when((b <= z) & (z < last))
        def _():
            hop(b, True).wait_send()

        @pl.when((b >= z) & (z > 0))
        def _():
            hop(b, False).wait_send()

        swap(b).wait_send()
        back(b, 1).wait_send()

        @pl.when(b != z)
        def _():
            back(b, 0).wait_send()


def run_experts(n, capacity, tokens, stream, codes, mix_hi, mix_lo, weights):
    rows, width = tokens.shape
    ffe = weights[2].shape[0]
    planes = n // 4
    n_experts = n // 2
    vmem = pl.BlockSpec(memory_space=pltpu.VMEM)
    anywhere = pl.BlockSpec(memory_space=pl.ANY)
    half = jnp.bfloat16
    dma = pltpu.SemaphoreType.DMA
    return pl.pallas_call(
        functools.partial(experts_kernel, n, capacity),
        out_shape=jax.ShapeDtypeStruct((rows, width), half),
        in_specs=[vmem] * 5 + [anywhere] * 6,
        out_specs=vmem,
        scratch_shapes=[
            pltpu.VMEM((planes, rows, width), half),
            pltpu.VMEM((planes, capacity, width), half),
            pltpu.VMEM((planes, capacity, width), half),
            pltpu.VMEM((2 * capacity, width), half),
            pltpu.VMEM((2 * capacity, 2 * ffe), half),
            pltpu.VMEM((planes, 2 * capacity, width), half),
            pltpu.VMEM((n_experts * capacity, width), half),
            pltpu.VMEM((width, 2 * ffe), half),
            pltpu.VMEM((width, 2 * ffe), half),
            pltpu.VMEM((2 * ffe, width), half),
            dma((6,)), dma((planes,)), dma((planes,)), dma((planes,)),
            dma((planes,)), dma((planes,)), dma((2 * planes,)), dma((n_experts,)),
        ],
        compiler_params=pltpu.CompilerParams(
            collective_id=1, has_side_effects=True, vmem_limit_bytes=56 * 1024 * 1024
        ),
        name="experts",
    )(tokens, stream, codes, mix_hi, mix_lo, *weights)


def local(
    queries, keys, values, segment_ids, residual, norm_gain, route_ids, route_weights,
    w_gate, w_up, w_down,
):
    rows, width = residual.shape
    n = lax.axis_size("ep")
    kv_heads = keys.shape[1] // HEAD_SIZE
    n_experts = n // 2
    topk = route_ids.shape[1]
    capacity = max(2, 2 * rows * topk // n_experts)

    swap = [(i, i ^ 1) for i in range(n)]
    other_gate = lax.ppermute(w_gate[0], "ep", swap)
    other_up = lax.ppermute(w_up[0], "ep", swap)
    other_down = lax.ppermute(w_down[0], "ep", swap)

    seg_row = jnp.zeros((SEG_ROWS, 2 * keys.shape[1]), jnp.bfloat16)
    seg_row = lax.dynamic_update_slice(
        seg_row, jnp.broadcast_to(segment_ids.astype(jnp.bfloat16)[None, :], (SEG_ROWS, rows)), (0, 0)
    )
    kv = jnp.concatenate([jnp.concatenate([keys, values], 1), seg_row], 0)
    segcol = segment_ids.astype(jnp.float32)[:, None]

    experts = jnp.arange(n_experts, dtype=jnp.int32)
    hit = route_ids[:, :, None] == experts[None, None, :]
    named = jnp.any(hit, 1)
    weight = jnp.sum(jnp.where(hit, route_weights[:, :, None], 0.0), 1)
    below = jnp.tril(jnp.ones((rows, rows), jnp.bfloat16), -1)
    slot = jnp.dot(below, named.astype(jnp.bfloat16), preferred_element_type=jnp.float32).astype(jnp.int32)
    code = jnp.where(named, slot, -1)
    slots = jnp.arange(capacity, dtype=jnp.int32)
    place = (code.T[:, None, :] == slots[None, :, None]).astype(jnp.bfloat16)
    place = place.reshape(n_experts * capacity, rows)
    mix = jnp.where(code[:, :, None] == slots[None, None, :], weight[:, :, None], 0.0)
    mix = mix.reshape(rows, n_experts * capacity)
    mix_hi = mix.astype(jnp.bfloat16)
    mix_lo = (mix - mix_hi.astype(jnp.float32)).astype(jnp.bfloat16)

    if n == 16:
        codes = lax.all_gather(code.T.astype(jnp.float32), "ep").reshape(n * n_experts, 1, rows)
        stream, normed = attention(n, kv_heads, queries, kv, segcol, residual, norm_gain[None, :])
        weights = (w_gate[0], w_up[0], w_down[0], other_gate, other_up, other_down)
        return run_experts(n, capacity, normed, stream, codes, mix_hi, mix_lo, weights)

    stream, outgoing = attention(n, kv_heads, queries, kv, segcol, residual, norm_gain[None, :], place)

    groups = [[c for c in range(k, n, 2)] for k in range(2)]
    arrived = lax.all_to_all(
        outgoing.reshape(n_experts, capacity, width), "ep", split_axis=0, concat_axis=0,
        axis_index_groups=groups, tiled=True,
    ).reshape(-1, width)

    def half(gate_half, up_half, down_half):
        gate = jnp.dot(arrived, gate_half, preferred_element_type=jnp.float32)
        upward = jnp.dot(arrived, up_half, preferred_element_type=jnp.float32)
        hidden = (jax.nn.silu(gate) * upward).astype(jnp.bfloat16)
        return jnp.dot(hidden, down_half, preferred_element_type=jnp.float32)

    out = half(w_gate[0], w_up[0], w_down[0]) + half(other_gate, other_up, other_down)
    returned = lax.all_to_all(
        out.astype(jnp.bfloat16).reshape(n_experts, capacity, width), "ep", split_axis=0,
        concat_axis=0, axis_index_groups=groups, tiled=True,
    ).reshape(-1, width)
    mixed = jnp.dot(mix_hi, returned, preferred_element_type=jnp.float32) + jnp.dot(
        mix_lo, returned, preferred_element_type=jnp.float32
    )
    return (stream.astype(jnp.float32) + mixed).astype(jnp.bfloat16)


def solution(mesh):
    tokens = P(("group", "ep"), None)
    split = P("ep", None, None)
    placed = (
        tokens, tokens, tokens, P(("group", "ep")), tokens, P(), tokens, tokens, split, split, split,
    )
    return jax.shard_map(local, mesh=mesh, in_specs=placed, out_specs=tokens, check_vma=False)
```

```python
import functools
import math

import jax
import jax.numpy as jnp
from jax import lax
from jax.experimental import pallas as pl
from jax.experimental.pallas import tpu as pltpu
from jax.sharding import PartitionSpec as P

HEAD_SIZE = 128
REACH = 8
NEGATIVE = -1e30
MESH = pl.DeviceIdType.MESH
SEG_ROWS = 16


def nt_dot(a, b):
    return lax.dot_general(a, b, (((1,), (1,)), ((), ())), preferred_element_type=jnp.float32)


def attention_kernel(
    n, kv_heads, placing, q_ref, kv_ref, segcol_ref, res_ref, gain_ref, *rest
):
    if placing:
        place_ref, stream_ref, rows_ref, held, bias, all_kv, attended, normed, send_sem, recv_sem = rest
    else:
        stream_ref, normed, held, bias, all_kv, attended, send_sem, recv_sem = rest
    me = lax.axis_index("ep")
    rows = q_ref.shape[0]
    heads = q_ref.shape[1] // HEAD_SIZE
    per_kv = heads // kv_heads
    reach = min(REACH, n - 1)

    barrier = pltpu.get_barrier_semaphore()
    for d in range(1, reach + 1):
        pl.semaphore_signal(
            barrier, inc=1, device_id={"ep": lax.rem(me + n - d, n)}, device_id_type=MESH
        )
    pl.semaphore_wait(barrier, reach)

    copies = []
    for d in range(1, reach + 1):
        copy = pltpu.make_async_remote_copy(
            src_ref=kv_ref, dst_ref=held.at[d],
            send_sem=send_sem.at[d], recv_sem=recv_sem.at[d],
            device_id={"ep": lax.rem(me + d, n)}, device_id_type=MESH,
        )
        copy.start()
        copies.append(copy)
    held[0] = kv_ref[...]
    for copy in copies:
        copy.wait()

    query_seg = segcol_ref[...]
    t = lax.broadcasted_iota(jnp.int32, (rows, rows), 0)
    u = lax.broadcasted_iota(jnp.int32, (rows, rows), 1)
    for d in range(reach + 1):
        key_seg = held[d, rows : rows + SEG_ROWS, 0:rows][0:1].astype(jnp.float32)
        allowed = (key_seg == query_seg) & (u - d * rows <= t) & (u + (me - d) * rows >= 0)
        bias[:, d * rows : (d + 1) * rows] = jnp.where(allowed, 0.0, NEGATIVE)
        for part in range(2 * kv_heads):
            all_kv[part, d * rows : (d + 1) * rows, :] = held[
                d, 0:rows, part * HEAD_SIZE : (part + 1) * HEAD_SIZE
            ]

    scale = math.log2(math.e) / math.sqrt(HEAD_SIZE)

    stack = 2

    def some_heads(h, g):
        cols = [
            pl.ds(pl.multiple_of((h + j) * HEAD_SIZE, HEAD_SIZE), HEAD_SIZE) for j in range(stack)
        ]
        q = jnp.concatenate([q_ref[:, col] for col in cols], 0)
        s = nt_dot(q, all_kv[g]) * scale
        s = (s.reshape(stack, rows, s.shape[1]) + bias[...][None]).reshape(s.shape)
        top = jnp.max(s, -1, keepdims=True)
        p = jnp.exp2(s - top)
        total = jnp.sum(p, -1, keepdims=True)
        pv = jnp.dot(
            p.astype(jnp.bfloat16), all_kv[kv_heads + g], preferred_element_type=jnp.float32
        )
        done = (pv / total).astype(jnp.bfloat16)
        for j, col in enumerate(cols):
            attended[:, col] = done[j * rows : (j + 1) * rows]

    def heads_step(i, carry):
        for g in range(kv_heads):
            some_heads(i * stack + g * per_kv, g)
        return carry

    lax.fori_loop(0, per_kv // stack, heads_step, 0)

    chunk = 16

    def norm_step(i, carry):
        r = pl.ds(pl.multiple_of(i * chunk, chunk), chunk)
        stream = (res_ref[r, :].astype(jnp.float32) + attended[r, :].astype(jnp.float32)).astype(
            jnp.bfloat16
        )
        stream_ref[r, :] = stream
        sf = stream.astype(jnp.float32)
        inv = lax.rsqrt(jnp.mean(sf * sf, -1, keepdims=True) + 1e-06)
        normed[r, :] = (sf * inv * gain_ref[...].astype(jnp.float32)).astype(jnp.bfloat16)
        return carry

    lax.fori_loop(0, rows // chunk, norm_step, 0)

    if not placing:
        return
    tile = 512

    def place_step(i, carry):
        c = pl.ds(pl.multiple_of(i * tile, tile), tile)
        rows_ref[:, c] = jnp.dot(
            place_ref[...], normed[:, c], preferred_element_type=jnp.float32
        ).astype(jnp.bfloat16)
        return carry

    lax.fori_loop(0, normed.shape[1] // tile, place_step, 0)


def attention(n, kv_heads, queries, kv, segcol, residual, gain, place=None):
    rows, width = queries.shape
    reach = min(REACH, n - 1)
    vmem = pl.BlockSpec(memory_space=pltpu.VMEM)
    placing = place is not None
    sent = place.shape[0] if placing else rows
    operands = (queries, kv, segcol, residual, gain) + ((place,) if placing else ())
    scratch = [
        pltpu.VMEM((reach + 1,) + kv.shape, jnp.bfloat16),
        pltpu.VMEM((rows, (reach + 1) * rows), jnp.float32),
        pltpu.VMEM((2 * kv_heads, (reach + 1) * rows, HEAD_SIZE), jnp.bfloat16),
        pltpu.VMEM((rows, width), jnp.bfloat16),
    ]
    if placing:
        scratch.append(pltpu.VMEM((rows, width), jnp.bfloat16))
    return pl.pallas_call(
        functools.partial(attention_kernel, n, kv_heads, placing),
        out_shape=(
            jax.ShapeDtypeStruct((rows, width), jnp.bfloat16),
            jax.ShapeDtypeStruct((sent, width), jnp.bfloat16),
        ),
        in_specs=[vmem] * len(operands),
        out_specs=(vmem, vmem),
        scratch_shapes=scratch + [
            pltpu.SemaphoreType.DMA((reach + 1,)),
            pltpu.SemaphoreType.DMA((reach + 1,)),
        ],
        compiler_params=pltpu.CompilerParams(
            collective_id=0, has_side_effects=True, vmem_limit_bytes=40 * 1024 * 1024
        ),
        name="attention",
    )(*operands)


def experts_kernel(
    n, capacity, tokens_ref, stream_ref, codes_ref, hi_ref, lo_ref,
    gate0, up0, down0, gate1, up1, down1,
    out_ref,
    line, codes, x_out, x_in, feed, hidden, result, returned, w_gate, w_up, w_down,
    w_sem, recv_sem, up_sem, down_sem, code_recv, code_up, code_down, x_send, x_recv, back_send, back_recv,
):
    planes = n // 4
    n_experts = n // 2
    last = planes - 1
    me = lax.axis_index("ep")
    z = me // 4
    x = lax.rem(me // 2, 2)
    c = lax.rem(me, 2)
    expert = me // 2
    partner = me + 2 - 4 * x
    partner_expert = expert + 1 - 2 * x
    rows, width = tokens_ref.shape
    ffe = down0.shape[0]

    barrier = pltpu.get_barrier_semaphore()
    for k in range(1, n_experts):
        pl.semaphore_signal(
            barrier, inc=1, device_id={"ep": lax.rem(me + 2 * k, n)}, device_id_type=MESH
        )

    loads = []
    for j, (g, u, d) in enumerate(((gate0, up0, down0), (gate1, up1, down1))):
        part = pl.ds(j * ffe, ffe)
        for k, (src, dst) in enumerate(
            ((g, w_gate.at[:, part]), (u, w_up.at[:, part]), (d, w_down.at[part, :]))
        ):
            load = pltpu.make_async_copy(src, dst, w_sem.at[3 * j + k])
            load.start()
            loads.append(load)

    line[z] = tokens_ref[...]
    codes[z] = codes_ref[...]
    pl.semaphore_wait(barrier, n_experts - 1)

    def hops(b, upward):
        target = {"ep": lax.rem(me + 4, n) if upward else lax.rem(me + n - 4, n)}
        return (
            pltpu.make_async_remote_copy(
                src_ref=codes.at[b], dst_ref=codes.at[b],
                send_sem=(code_up if upward else code_down).at[b], recv_sem=code_recv.at[b],
                device_id=target, device_id_type=MESH,
            ),
            pltpu.make_async_remote_copy(
                src_ref=line.at[b], dst_ref=line.at[b],
                send_sem=(up_sem if upward else down_sem).at[b], recv_sem=recv_sem.at[b],
                device_id=target, device_id_type=MESH,
            ),
        )

    def swap(b):
        return pltpu.make_async_remote_copy(
            src_ref=x_out.at[b], dst_ref=x_in.at[b],
            send_sem=x_send.at[b], recv_sem=x_recv.at[b],
            device_id={"ep": partner}, device_id_type=MESH,
        )

    def back(b, other):
        side = 1 - x if other else x
        return pltpu.make_async_remote_copy(
            src_ref=result.at[b, pl.ds(capacity * other, capacity)],
            dst_ref=returned.at[pl.ds(pl.multiple_of(expert * capacity, capacity), capacity)],
            send_sem=back_send.at[2 * b + other], recv_sem=back_recv.at[expert],
            device_id={"ep": b * 4 + side * 2 + c}, device_id_type=MESH,
        )

    slots = lax.broadcasted_iota(jnp.int32, (capacity, rows), 0).astype(jnp.float32)
    tile = 512
    tiles = width // tile

    def pack(b, e, put):
        place = (codes[b, e] == slots).astype(jnp.bfloat16)

        def step(i, carry):
            col = pl.ds(pl.multiple_of(i * tile, tile), tile)
            put(col, jnp.dot(
                place, line[b, :, col], preferred_element_type=jnp.float32
            ).astype(jnp.bfloat16))
            return carry

        lax.fori_loop(0, tiles, step, 0)

    def arrive(b):
        @pl.when(b != z)
        def _():
            for copy in hops(b, True):
                copy.wait_recv()

        @pl.when((b <= z) & (z < last))
        def _():
            for copy in hops(b, True):
                copy.start()

        @pl.when((b >= z) & (z > 0))
        def _():
            for copy in hops(b, False):
                copy.start()

        def put(col, value):
            x_out[b, :, col] = value

        pack(b, partner_expert, put)
        swap(b).start()

    def order(i):
        low = jnp.minimum(z, last - z)
        b = jnp.where((low == 1) & (i < 3), lax.rem(i + 1, 3), i)
        return jnp.where(z < planes // 2, b, last - b)

    def put_feed(col, value):
        feed[0:capacity, col] = value

    hidden_tile = 256

    def step(i, carry):
        b = order(i)
        inner = (z > 0) & (z < last)

        @pl.when((i != 2) | jnp.logical_not(inner))
        def _():
            arrive(b)

        @pl.when((i == 1) & inner)
        def _():
            arrive(order(2))

        pack(b, expert, put_feed)

        @pl.when(i == 0)
        def _():
            for load in loads:
                load.wait()

        swap(b).wait_recv()
        feed[capacity : 2 * capacity, :] = x_in[b]

        def hidden_step(k, inner_carry):
            col = pl.ds(pl.multiple_of(k * hidden_tile, hidden_tile), hidden_tile)
            gate = jnp.dot(feed[...], w_gate[:, col], preferred_element_type=jnp.float32)
            upward = jnp.dot(feed[...], w_up[:, col], preferred_element_type=jnp.float32)
            hidden[:, col] = (jax.nn.silu(gate) * upward).astype(jnp.bfloat16)
            return inner_carry

        lax.fori_loop(0, 2 * ffe // hidden_tile, hidden_step, 0)

        def down_step(k, inner_carry):
            col = pl.ds(pl.multiple_of(k * tile, tile), tile)
            result[b, :, col] = jnp.dot(
                hidden[...], w_down[:, col], preferred_element_type=jnp.float32
            ).astype(jnp.bfloat16)
            return inner_carry

        lax.fori_loop(0, tiles, down_step, 0)

        back(b, 1).start()

        @pl.when(b != z)
        def _():
            back(b, 0).start()

        @pl.when(b == z)
        def _():
            returned[pl.ds(pl.multiple_of(expert * capacity, capacity), capacity), :] = result[
                b, 0:capacity
            ]

        return carry

    lax.fori_loop(0, planes, step, 0)

    for e in range(n_experts):
        @pl.when(expert != e)
        def _():
            pltpu.make_async_remote_copy(
                src_ref=result.at[0, pl.ds(0, capacity)],
                dst_ref=returned.at[pl.ds(e * capacity, capacity)],
                send_sem=back_send.at[0], recv_sem=back_recv.at[e],
                device_id={"ep": partner}, device_id_type=MESH,
            ).wait_recv()

    def mix_step(i, carry):
        col = pl.ds(pl.multiple_of(i * tile, tile), tile)
        picked = returned[:, col]
        mixed = jnp.dot(hi_ref[...], picked, preferred_element_type=jnp.float32)
        mixed += jnp.dot(lo_ref[...], picked, preferred_element_type=jnp.float32)
        out_ref[:, col] = (stream_ref[:, col].astype(jnp.float32) + mixed).astype(jnp.bfloat16)
        return carry

    lax.fori_loop(0, tiles, mix_step, 0)

    for b in range(planes):
        @pl.when((b <= z) & (z < last))
        def _():
            for copy in hops(b, True):
                copy.wait_send()

        @pl.when((b >= z) & (z > 0))
        def _():
            for copy in hops(b, False):
                copy.wait_send()

        swap(b).wait_send()
        back(b, 1).wait_send()

        @pl.when(b != z)
        def _():
            back(b, 0).wait_send()


def run_experts(n, capacity, tokens, stream, codes, mix_hi, mix_lo, weights):
    rows, width = tokens.shape
    ffe = weights[2].shape[0]
    planes = n // 4
    n_experts = n // 2
    vmem = pl.BlockSpec(memory_space=pltpu.VMEM)
    anywhere = pl.BlockSpec(memory_space=pl.ANY)
    half = jnp.bfloat16
    dma = pltpu.SemaphoreType.DMA
    return pl.pallas_call(
        functools.partial(experts_kernel, n, capacity),
        out_shape=jax.ShapeDtypeStruct((rows, width), half),
        in_specs=[vmem] * 5 + [anywhere] * 6,
        out_specs=vmem,
        scratch_shapes=[
            pltpu.VMEM((planes, rows, width), half),
            pltpu.VMEM((planes, n_experts, 1, rows), jnp.float32),
            pltpu.VMEM((planes, capacity, width), half),
            pltpu.VMEM((planes, capacity, width), half),
            pltpu.VMEM((2 * capacity, width), half),
            pltpu.VMEM((2 * capacity, 2 * ffe), half),
            pltpu.VMEM((planes, 2 * capacity, width), half),
            pltpu.VMEM((n_experts * capacity, width), half),
            pltpu.VMEM((width, 2 * ffe), half),
            pltpu.VMEM((width, 2 * ffe), half),
            pltpu.VMEM((2 * ffe, width), half),
            dma((6,)), dma((planes,)), dma((planes,)), dma((planes,)),
            dma((planes,)), dma((planes,)), dma((planes,)),
            dma((planes,)), dma((planes,)), dma((2 * planes,)), dma((n_experts,)),
        ],
        compiler_params=pltpu.CompilerParams(
            collective_id=1, has_side_effects=True, vmem_limit_bytes=56 * 1024 * 1024
        ),
        name="experts",
    )(tokens, stream, codes, mix_hi, mix_lo, *weights)


def local(
    queries, keys, values, segment_ids, residual, norm_gain, route_ids, route_weights,
    w_gate, w_up, w_down,
):
    rows, width = residual.shape
    n = lax.axis_size("ep")
    kv_heads = keys.shape[1] // HEAD_SIZE
    n_experts = n // 2
    topk = route_ids.shape[1]
    capacity = max(2, 2 * rows * topk // n_experts)

    swap = [(i, i ^ 1) for i in range(n)]
    other_gate = lax.ppermute(w_gate[0], "ep", swap)
    other_up = lax.ppermute(w_up[0], "ep", swap)
    other_down = lax.ppermute(w_down[0], "ep", swap)

    seg_row = jnp.zeros((SEG_ROWS, 2 * keys.shape[1]), jnp.bfloat16)
    seg_row = lax.dynamic_update_slice(
        seg_row, jnp.broadcast_to(segment_ids.astype(jnp.bfloat16)[None, :], (SEG_ROWS, rows)), (0, 0)
    )
    kv = jnp.concatenate([jnp.concatenate([keys, values], 1), seg_row], 0)
    segcol = segment_ids.astype(jnp.float32)[:, None]

    experts = jnp.arange(n_experts, dtype=jnp.int32)
    hit = route_ids[:, :, None] == experts[None, None, :]
    named = jnp.any(hit, 1)
    weight = jnp.sum(jnp.where(hit, route_weights[:, :, None], 0.0), 1)
    below = jnp.tril(jnp.ones((rows, rows), jnp.bfloat16), -1)
    slot = jnp.dot(below, named.astype(jnp.bfloat16), preferred_element_type=jnp.float32).astype(jnp.int32)
    code = jnp.where(named, slot, -1)
    slots = jnp.arange(capacity, dtype=jnp.int32)
    place = (code.T[:, None, :] == slots[None, :, None]).astype(jnp.bfloat16)
    place = place.reshape(n_experts * capacity, rows)
    mix = jnp.where(code[:, :, None] == slots[None, None, :], weight[:, :, None], 0.0)
    mix = mix.reshape(rows, n_experts * capacity)
    mix_hi = mix.astype(jnp.bfloat16)
    mix_lo = (mix - mix_hi.astype(jnp.float32)).astype(jnp.bfloat16)

    if n == 16:
        codes = code.T.astype(jnp.float32).reshape(n_experts, 1, rows)
        stream, normed = attention(n, kv_heads, queries, kv, segcol, residual, norm_gain[None, :])
        weights = (w_gate[0], w_up[0], w_down[0], other_gate, other_up, other_down)
        return run_experts(n, capacity, normed, stream, codes, mix_hi, mix_lo, weights)

    stream, outgoing = attention(n, kv_heads, queries, kv, segcol, residual, norm_gain[None, :], place)

    groups = [[c for c in range(k, n, 2)] for k in range(2)]
    arrived = lax.all_to_all(
        outgoing.reshape(n_experts, capacity, width), "ep", split_axis=0, concat_axis=0,
        axis_index_groups=groups, tiled=True,
    ).reshape(-1, width)

    def half(gate_half, up_half, down_half):
        gate = jnp.dot(arrived, gate_half, preferred_element_type=jnp.float32)
        upward = jnp.dot(arrived, up_half, preferred_element_type=jnp.float32)
        hidden = (jax.nn.silu(gate) * upward).astype(jnp.bfloat16)
        return jnp.dot(hidden, down_half, preferred_element_type=jnp.float32)

    out = half(w_gate[0], w_up[0], w_down[0]) + half(other_gate, other_up, other_down)
    returned = lax.all_to_all(
        out.astype(jnp.bfloat16).reshape(n_experts, capacity, width), "ep", split_axis=0,
        concat_axis=0, axis_index_groups=groups, tiled=True,
    ).reshape(-1, width)
    mixed = jnp.dot(mix_hi, returned, preferred_element_type=jnp.float32) + jnp.dot(
        mix_lo, returned, preferred_element_type=jnp.float32
    )
    return (stream.astype(jnp.float32) + mixed).astype(jnp.bfloat16)


def solution(mesh):
    tokens = P(("group", "ep"), None)
    split = P("ep", None, None)
    placed = (
        tokens, tokens, tokens, P(("group", "ep")), tokens, P(), tokens, tokens, split, split, split,
    )
    return jax.shard_map(local, mesh=mesh, in_specs=placed, out_specs=tokens, check_vma=False)
```

```python
import functools
import math

import jax
import jax.numpy as jnp
from jax import lax
from jax.experimental import pallas as pl
from jax.experimental.pallas import tpu as pltpu
from jax.sharding import PartitionSpec as P

HEAD_SIZE = 128
REACH = 8
NEGATIVE = -1e30
MESH = pl.DeviceIdType.MESH
SEG_ROWS = 16


def nt_dot(a, b):
    return lax.dot_general(a, b, (((1,), (1,)), ((), ())), preferred_element_type=jnp.float32)


def attention_kernel(
    n, kv_heads, placing, q_ref, kv_ref, segcol_ref, res_ref, gain_ref, *rest
):
    if placing:
        place_ref, stream_ref, rows_ref, held, bias, all_kv, attended, normed, send_sem, recv_sem = rest
    else:
        stream_ref, normed, held, bias, all_kv, attended, send_sem, recv_sem = rest
    me = lax.axis_index("ep")
    rows = q_ref.shape[0]
    heads = q_ref.shape[1] // HEAD_SIZE
    per_kv = heads // kv_heads
    reach = min(REACH, n - 1)

    barrier = pltpu.get_barrier_semaphore()
    for d in range(1, reach + 1):
        pl.semaphore_signal(
            barrier, inc=1, device_id={"ep": lax.rem(me + n - d, n)}, device_id_type=MESH
        )
    pl.semaphore_wait(barrier, reach)

    copies = []
    for d in range(1, reach + 1):
        copy = pltpu.make_async_remote_copy(
            src_ref=kv_ref, dst_ref=held.at[d],
            send_sem=send_sem.at[d], recv_sem=recv_sem.at[d],
            device_id={"ep": lax.rem(me + d, n)}, device_id_type=MESH,
        )
        copy.start()
        copies.append(copy)
    held[0] = kv_ref[...]
    for copy in copies:
        copy.wait()

    query_seg = segcol_ref[...]
    t = lax.broadcasted_iota(jnp.int32, (rows, rows), 0)
    u = lax.broadcasted_iota(jnp.int32, (rows, rows), 1)
    for d in range(reach + 1):
        key_seg = held[d, rows : rows + SEG_ROWS, 0:rows][0:1].astype(jnp.float32)
        allowed = (key_seg == query_seg) & (u - d * rows <= t) & (u + (me - d) * rows >= 0)
        bias[:, d * rows : (d + 1) * rows] = jnp.where(allowed, 0.0, NEGATIVE)
        for part in range(2 * kv_heads):
            all_kv[part, d * rows : (d + 1) * rows, :] = held[
                d, 0:rows, part * HEAD_SIZE : (part + 1) * HEAD_SIZE
            ]

    scale = math.log2(math.e) / math.sqrt(HEAD_SIZE)

    stack = 2

    def some_heads(h, g):
        cols = [
            pl.ds(pl.multiple_of((h + j) * HEAD_SIZE, HEAD_SIZE), HEAD_SIZE) for j in range(stack)
        ]
        q = jnp.concatenate([q_ref[:, col] for col in cols], 0)
        s = nt_dot(q, all_kv[g]) * scale
        s = (s.reshape(stack, rows, s.shape[1]) + bias[...][None]).reshape(s.shape)
        top = jnp.max(s, -1, keepdims=True)
        p = jnp.exp2(s - top)
        total = jnp.sum(p, -1, keepdims=True)
        pv = jnp.dot(
            p.astype(jnp.bfloat16), all_kv[kv_heads + g], preferred_element_type=jnp.float32
        )
        done = (pv / total).astype(jnp.bfloat16)
        for j, col in enumerate(cols):
            attended[:, col] = done[j * rows : (j + 1) * rows]

    def heads_step(i, carry):
        for g in range(kv_heads):
            some_heads(i * stack + g * per_kv, g)
        return carry

    lax.fori_loop(0, per_kv // stack, heads_step, 0)

    chunk = 16

    def norm_step(i, carry):
        r = pl.ds(pl.multiple_of(i * chunk, chunk), chunk)
        stream = (res_ref[r, :].astype(jnp.float32) + attended[r, :].astype(jnp.float32)).astype(
            jnp.bfloat16
        )
        stream_ref[r, :] = stream
        sf = stream.astype(jnp.float32)
        inv = lax.rsqrt(jnp.mean(sf * sf, -1, keepdims=True) + 1e-06)
        normed[r, :] = (sf * inv * gain_ref[...].astype(jnp.float32)).astype(jnp.bfloat16)
        return carry

    lax.fori_loop(0, rows // chunk, norm_step, 0)

    if not placing:
        return
    tile = 512

    def place_step(i, carry):
        c = pl.ds(pl.multiple_of(i * tile, tile), tile)
        rows_ref[:, c] = jnp.dot(
            place_ref[...], normed[:, c], preferred_element_type=jnp.float32
        ).astype(jnp.bfloat16)
        return carry

    lax.fori_loop(0, normed.shape[1] // tile, place_step, 0)


def attention(n, kv_heads, queries, kv, segcol, residual, gain, place=None):
    rows, width = queries.shape
    reach = min(REACH, n - 1)
    vmem = pl.BlockSpec(memory_space=pltpu.VMEM)
    placing = place is not None
    sent = place.shape[0] if placing else rows
    operands = (queries, kv, segcol, residual, gain) + ((place,) if placing else ())
    scratch = [
        pltpu.VMEM((reach + 1,) + kv.shape, jnp.bfloat16),
        pltpu.VMEM((rows, (reach + 1) * rows), jnp.float32),
        pltpu.VMEM((2 * kv_heads, (reach + 1) * rows, HEAD_SIZE), jnp.bfloat16),
        pltpu.VMEM((rows, width), jnp.bfloat16),
    ]
    if placing:
        scratch.append(pltpu.VMEM((rows, width), jnp.bfloat16))
    return pl.pallas_call(
        functools.partial(attention_kernel, n, kv_heads, placing),
        out_shape=(
            jax.ShapeDtypeStruct((rows, width), jnp.bfloat16),
            jax.ShapeDtypeStruct((sent, width), jnp.bfloat16),
        ),
        in_specs=[vmem] * len(operands),
        out_specs=(vmem, vmem),
        scratch_shapes=scratch + [
            pltpu.SemaphoreType.DMA((reach + 1,)),
            pltpu.SemaphoreType.DMA((reach + 1,)),
        ],
        compiler_params=pltpu.CompilerParams(
            collective_id=0, has_side_effects=True, vmem_limit_bytes=40 * 1024 * 1024
        ),
        name="attention",
    )(*operands)


def experts_kernel(
    n, capacity, tokens_ref, stream_ref, codes_ref, hi_ref, lo_ref,
    gate0, up0, down0, gate1, up1, down1,
    out_ref,
    line, codes, x_out, x_in, feed, hidden, result, returned, w_gate, w_up, w_down,
    w_sem, recv_sem, up_sem, down_sem, code_recv, code_up, code_down, x_send, x_recv, back_send, back_recv,
):
    planes = n // 4
    n_experts = n // 2
    last = planes - 1
    me = lax.axis_index("ep")
    z = me // 4
    x = lax.rem(me // 2, 2)
    c = lax.rem(me, 2)
    expert = me // 2
    partner = me + 2 - 4 * x
    partner_expert = expert + 1 - 2 * x
    rows, width = tokens_ref.shape
    ffe = down0.shape[0]

    barrier = pltpu.get_barrier_semaphore()
    for k in range(1, n_experts):
        pl.semaphore_signal(
            barrier, inc=1, device_id={"ep": lax.rem(me + 2 * k, n)}, device_id_type=MESH
        )

    loads = []
    for j, (g, u, d) in enumerate(((gate0, up0, down0), (gate1, up1, down1))):
        part = pl.ds(j * ffe, ffe)
        for k, (src, dst) in enumerate(
            ((g, w_gate.at[:, part]), (u, w_up.at[:, part]), (d, w_down.at[part, :]))
        ):
            load = pltpu.make_async_copy(src, dst, w_sem.at[3 * j + k])
            load.start()
            loads.append(load)

    line[z] = tokens_ref[...]
    codes[z] = codes_ref[...]
    pl.semaphore_wait(barrier, n_experts - 1)

    def hops(b, upward):
        target = {"ep": lax.rem(me + 4, n) if upward else lax.rem(me + n - 4, n)}
        return (
            pltpu.make_async_remote_copy(
                src_ref=codes.at[b], dst_ref=codes.at[b],
                send_sem=(code_up if upward else code_down).at[b], recv_sem=code_recv.at[b],
                device_id=target, device_id_type=MESH,
            ),
            pltpu.make_async_remote_copy(
                src_ref=line.at[b], dst_ref=line.at[b],
                send_sem=(up_sem if upward else down_sem).at[b], recv_sem=recv_sem.at[b],
                device_id=target, device_id_type=MESH,
            ),
        )

    def swap(b):
        return pltpu.make_async_remote_copy(
            src_ref=x_out.at[b], dst_ref=x_in.at[b],
            send_sem=x_send.at[b], recv_sem=x_recv.at[b],
            device_id={"ep": partner}, device_id_type=MESH,
        )

    def back(b, other):
        side = 1 - x if other else x
        return pltpu.make_async_remote_copy(
            src_ref=result.at[b, pl.ds(capacity * other, capacity)],
            dst_ref=returned.at[pl.ds(pl.multiple_of(expert * capacity, capacity), capacity)],
            send_sem=back_send.at[2 * b + other], recv_sem=back_recv.at[expert],
            device_id={"ep": b * 4 + side * 2 + c}, device_id_type=MESH,
        )

    slots = lax.broadcasted_iota(jnp.int32, (capacity, rows), 0).astype(jnp.float32)
    tile = 512
    tiles = width // tile

    def pack(b, e, put):
        place = (codes[b, e] == slots).astype(jnp.bfloat16)

        def step(i, carry):
            col = pl.ds(pl.multiple_of(i * tile, tile), tile)
            put(col, jnp.dot(
                place, line[b, :, col], preferred_element_type=jnp.float32
            ).astype(jnp.bfloat16))
            return carry

        lax.fori_loop(0, tiles, step, 0)

    def arrive(b):
        @pl.when(b != z)
        def _():
            for copy in hops(b, True):
                copy.wait_recv()

        @pl.when((b <= z) & (z < last))
        def _():
            for copy in hops(b, True):
                copy.start()

        @pl.when((b >= z) & (z > 0))
        def _():
            for copy in hops(b, False):
                copy.start()

        def put(col, value):
            x_out[b, :, col] = value

        pack(b, partner_expert, put)
        swap(b).start()

    def order(i):
        low = jnp.minimum(z, last - z)
        b = jnp.where((low == 1) & (i < 2), 1 - i, i)
        return jnp.where(z < planes // 2, b, last - b)

    def put_feed(col, value):
        feed[0:capacity, col] = value

    hidden_tile = 256

    def step(i, carry):
        b = order(i)
        inner = (z > 0) & (z < last)

        @pl.when((i != 2) | jnp.logical_not(inner))
        def _():
            arrive(b)

        @pl.when((i == 1) & inner)
        def _():
            arrive(order(2))

        pack(b, expert, put_feed)

        @pl.when(i == 0)
        def _():
            for load in loads:
                load.wait()

        swap(b).wait_recv()
        feed[capacity : 2 * capacity, :] = x_in[b]

        def hidden_step(k, inner_carry):
            col = pl.ds(pl.multiple_of(k * hidden_tile, hidden_tile), hidden_tile)
            gate = jnp.dot(feed[...], w_gate[:, col], preferred_element_type=jnp.float32)
            upward = jnp.dot(feed[...], w_up[:, col], preferred_element_type=jnp.float32)
            hidden[:, col] = (jax.nn.silu(gate) * upward).astype(jnp.bfloat16)
            return inner_carry

        lax.fori_loop(0, 2 * ffe // hidden_tile, hidden_step, 0)

        def down_step(k, inner_carry):
            col = pl.ds(pl.multiple_of(k * tile, tile), tile)
            result[b, :, col] = jnp.dot(
                hidden[...], w_down[:, col], preferred_element_type=jnp.float32
            ).astype(jnp.bfloat16)
            return inner_carry

        lax.fori_loop(0, tiles, down_step, 0)

        back(b, 1).start()

        @pl.when(b != z)
        def _():
            back(b, 0).start()

        @pl.when(b == z)
        def _():
            returned[pl.ds(pl.multiple_of(expert * capacity, capacity), capacity), :] = result[
                b, 0:capacity
            ]

        return carry

    lax.fori_loop(0, planes, step, 0)

    for e in range(n_experts):
        @pl.when(expert != e)
        def _():
            pltpu.make_async_remote_copy(
                src_ref=result.at[0, pl.ds(0, capacity)],
                dst_ref=returned.at[pl.ds(e * capacity, capacity)],
                send_sem=back_send.at[0], recv_sem=back_recv.at[e],
                device_id={"ep": partner}, device_id_type=MESH,
            ).wait_recv()

    def mix_step(i, carry):
        col = pl.ds(pl.multiple_of(i * tile, tile), tile)
        picked = returned[:, col]
        mixed = jnp.dot(hi_ref[...], picked, preferred_element_type=jnp.float32)
        mixed += jnp.dot(lo_ref[...], picked, preferred_element_type=jnp.float32)
        out_ref[:, col] = (stream_ref[:, col].astype(jnp.float32) + mixed).astype(jnp.bfloat16)
        return carry

    lax.fori_loop(0, tiles, mix_step, 0)

    for b in range(planes):
        @pl.when((b <= z) & (z < last))
        def _():
            for copy in hops(b, True):
                copy.wait_send()

        @pl.when((b >= z) & (z > 0))
        def _():
            for copy in hops(b, False):
                copy.wait_send()

        swap(b).wait_send()
        back(b, 1).wait_send()

        @pl.when(b != z)
        def _():
            back(b, 0).wait_send()


def run_experts(n, capacity, tokens, stream, codes, mix_hi, mix_lo, weights):
    rows, width = tokens.shape
    ffe = weights[2].shape[0]
    planes = n // 4
    n_experts = n // 2
    vmem = pl.BlockSpec(memory_space=pltpu.VMEM)
    anywhere = pl.BlockSpec(memory_space=pl.ANY)
    half = jnp.bfloat16
    dma = pltpu.SemaphoreType.DMA
    return pl.pallas_call(
        functools.partial(experts_kernel, n, capacity),
        out_shape=jax.ShapeDtypeStruct((rows, width), half),
        in_specs=[vmem] * 5 + [anywhere] * 6,
        out_specs=vmem,
        scratch_shapes=[
            pltpu.VMEM((planes, rows, width), half),
            pltpu.VMEM((planes, n_experts, 1, rows), jnp.float32),
            pltpu.VMEM((planes, capacity, width), half),
            pltpu.VMEM((planes, capacity, width), half),
            pltpu.VMEM((2 * capacity, width), half),
            pltpu.VMEM((2 * capacity, 2 * ffe), half),
            pltpu.VMEM((planes, 2 * capacity, width), half),
            pltpu.VMEM((n_experts * capacity, width), half),
            pltpu.VMEM((width, 2 * ffe), half),
            pltpu.VMEM((width, 2 * ffe), half),
            pltpu.VMEM((2 * ffe, width), half),
            dma((6,)), dma((planes,)), dma((planes,)), dma((planes,)),
            dma((planes,)), dma((planes,)), dma((planes,)),
            dma((planes,)), dma((planes,)), dma((2 * planes,)), dma((n_experts,)),
        ],
        compiler_params=pltpu.CompilerParams(
            collective_id=1, has_side_effects=True, vmem_limit_bytes=56 * 1024 * 1024
        ),
        name="experts",
    )(tokens, stream, codes, mix_hi, mix_lo, *weights)


def local(
    queries, keys, values, segment_ids, residual, norm_gain, route_ids, route_weights,
    w_gate, w_up, w_down,
):
    rows, width = residual.shape
    n = lax.axis_size("ep")
    kv_heads = keys.shape[1] // HEAD_SIZE
    n_experts = n // 2
    topk = route_ids.shape[1]
    capacity = max(2, 2 * rows * topk // n_experts)

    swap = [(i, i ^ 1) for i in range(n)]
    other_gate = lax.ppermute(w_gate[0], "ep", swap)
    other_up = lax.ppermute(w_up[0], "ep", swap)
    other_down = lax.ppermute(w_down[0], "ep", swap)

    seg_row = jnp.zeros((SEG_ROWS, 2 * keys.shape[1]), jnp.bfloat16)
    seg_row = lax.dynamic_update_slice(
        seg_row, jnp.broadcast_to(segment_ids.astype(jnp.bfloat16)[None, :], (SEG_ROWS, rows)), (0, 0)
    )
    kv = jnp.concatenate([jnp.concatenate([keys, values], 1), seg_row], 0)
    segcol = segment_ids.astype(jnp.float32)[:, None]

    experts = jnp.arange(n_experts, dtype=jnp.int32)
    hit = route_ids[:, :, None] == experts[None, None, :]
    named = jnp.any(hit, 1)
    weight = jnp.sum(jnp.where(hit, route_weights[:, :, None], 0.0), 1)
    below = jnp.tril(jnp.ones((rows, rows), jnp.bfloat16), -1)
    slot = jnp.dot(below, named.astype(jnp.bfloat16), preferred_element_type=jnp.float32).astype(jnp.int32)
    code = jnp.where(named, slot, -1)
    slots = jnp.arange(capacity, dtype=jnp.int32)
    place = (code.T[:, None, :] == slots[None, :, None]).astype(jnp.bfloat16)
    place = place.reshape(n_experts * capacity, rows)
    mix = jnp.where(code[:, :, None] == slots[None, None, :], weight[:, :, None], 0.0)
    mix = mix.reshape(rows, n_experts * capacity)
    mix_hi = mix.astype(jnp.bfloat16)
    mix_lo = (mix - mix_hi.astype(jnp.float32)).astype(jnp.bfloat16)

    if n == 16:
        codes = code.T.astype(jnp.float32).reshape(n_experts, 1, rows)
        stream, normed = attention(n, kv_heads, queries, kv, segcol, residual, norm_gain[None, :])
        weights = (w_gate[0], w_up[0], w_down[0], other_gate, other_up, other_down)
        return run_experts(n, capacity, normed, stream, codes, mix_hi, mix_lo, weights)

    stream, outgoing = attention(n, kv_heads, queries, kv, segcol, residual, norm_gain[None, :], place)

    groups = [[c for c in range(k, n, 2)] for k in range(2)]
    arrived = lax.all_to_all(
        outgoing.reshape(n_experts, capacity, width), "ep", split_axis=0, concat_axis=0,
        axis_index_groups=groups, tiled=True,
    ).reshape(-1, width)

    def half(gate_half, up_half, down_half):
        gate = jnp.dot(arrived, gate_half, preferred_element_type=jnp.float32)
        upward = jnp.dot(arrived, up_half, preferred_element_type=jnp.float32)
        hidden = (jax.nn.silu(gate) * upward).astype(jnp.bfloat16)
        return jnp.dot(hidden, down_half, preferred_element_type=jnp.float32)

    out = half(w_gate[0], w_up[0], w_down[0]) + half(other_gate, other_up, other_down)
    returned = lax.all_to_all(
        out.astype(jnp.bfloat16).reshape(n_experts, capacity, width), "ep", split_axis=0,
        concat_axis=0, axis_index_groups=groups, tiled=True,
    ).reshape(-1, width)
    mixed = jnp.dot(mix_hi, returned, preferred_element_type=jnp.float32) + jnp.dot(
        mix_lo, returned, preferred_element_type=jnp.float32
    )
    return (stream.astype(jnp.float32) + mixed).astype(jnp.bfloat16)


def solution(mesh):
    tokens = P(("group", "ep"), None)
    split = P("ep", None, None)
    placed = (
        tokens, tokens, tokens, P(("group", "ep")), tokens, P(), tokens, tokens, split, split, split,
    )
    return jax.shard_map(local, mesh=mesh, in_specs=placed, out_specs=tokens, check_vma=False)
```

```python
import functools
import math

import jax
import jax.numpy as jnp
from jax import lax
from jax.experimental import pallas as pl
from jax.experimental.pallas import tpu as pltpu
from jax.sharding import PartitionSpec as P

HEAD_SIZE = 128
REACH = 8
NEGATIVE = -1e30
MESH = pl.DeviceIdType.MESH
SEG_ROWS = 16


def nt_dot(a, b):
    return lax.dot_general(a, b, (((1,), (1,)), ((), ())), preferred_element_type=jnp.float32)


def attention_kernel(
    n, kv_heads, placing, q_ref, kv_ref, segcol_ref, res_ref, gain_ref, *rest
):
    if placing:
        place_ref, stream_ref, rows_ref, held, bias, all_kv, attended, normed, send_sem, recv_sem = rest
    else:
        stream_ref, normed, held, bias, all_kv, attended, send_sem, recv_sem = rest
    me = lax.axis_index("ep")
    rows = q_ref.shape[0]
    heads = q_ref.shape[1] // HEAD_SIZE
    per_kv = heads // kv_heads
    reach = min(REACH, n - 2)

    core = lax.rem(me, 2)
    sibling = me + 1 - 2 * core
    steps = range(2, reach + 1, 2)

    barrier = pltpu.get_barrier_semaphore()
    for d in steps:
        pl.semaphore_signal(
            barrier, inc=1, device_id={"ep": lax.rem(me + n - d, n)}, device_id_type=MESH
        )
    pl.semaphore_signal(barrier, inc=1, device_id={"ep": sibling}, device_id_type=MESH)
    pl.semaphore_wait(barrier, len(steps) + 1)

    def direct(d):
        return pltpu.make_async_remote_copy(
            src_ref=kv_ref, dst_ref=held.at[d],
            send_sem=send_sem.at[d], recv_sem=recv_sem.at[d],
            device_id={"ep": lax.rem(me + d, n)}, device_id_type=MESH,
        )

    def passed_on(k):
        return pltpu.make_async_remote_copy(
            src_ref=held.at[2 * k + 2 * core], dst_ref=held.at[2 * k + 1],
            send_sem=send_sem.at[2 * k + 1], recv_sem=recv_sem.at[2 * k + 1],
            device_id={"ep": sibling}, device_id_type=MESH,
        )

    for d in steps:
        direct(d).start()
    held[0] = kv_ref[...]
    for k in range(reach // 2):
        if k == 0:
            @pl.when(core == 1)
            def _():
                direct(2).wait_recv()
        else:
            direct(2 * k + 2 * core).wait_recv()
        passed_on(k).start()

    @pl.when(core == 0)
    def _():
        direct(reach).wait_recv()

    for k in range(reach // 2):
        passed_on(k).wait()
    for d in steps:
        direct(d).wait_send()

    query_seg = segcol_ref[...]
    t = lax.broadcasted_iota(jnp.int32, (rows, rows), 0)
    u = lax.broadcasted_iota(jnp.int32, (rows, rows), 1)
    for d in range(reach + 1):
        key_seg = held[d, rows : rows + SEG_ROWS, 0:rows][0:1].astype(jnp.float32)
        allowed = (key_seg == query_seg) & (u - d * rows <= t) & (u + (me - d) * rows >= 0)
        bias[:, d * rows : (d + 1) * rows] = jnp.where(allowed, 0.0, NEGATIVE)
        for part in range(2 * kv_heads):
            all_kv[part, d * rows : (d + 1) * rows, :] = held[
                d, 0:rows, part * HEAD_SIZE : (part + 1) * HEAD_SIZE
            ]

    scale = math.log2(math.e) / math.sqrt(HEAD_SIZE)

    stack = 2

    def some_heads(h, g):
        cols = [
            pl.ds(pl.multiple_of((h + j) * HEAD_SIZE, HEAD_SIZE), HEAD_SIZE) for j in range(stack)
        ]
        q = jnp.concatenate([q_ref[:, col] for col in cols], 0)
        s = nt_dot(q, all_kv[g]) * scale
        s = (s.reshape(stack, rows, s.shape[1]) + bias[...][None]).reshape(s.shape)
        top = jnp.max(s, -1, keepdims=True)
        p = jnp.exp2(s - top)
        total = jnp.sum(p, -1, keepdims=True)
        pv = jnp.dot(
            p.astype(jnp.bfloat16), all_kv[kv_heads + g], preferred_element_type=jnp.float32
        )
        done = (pv / total).astype(jnp.bfloat16)
        for j, col in enumerate(cols):
            attended[:, col] = done[j * rows : (j + 1) * rows]

    def heads_step(i, carry):
        for g in range(kv_heads):
            some_heads(i * stack + g * per_kv, g)
        return carry

    lax.fori_loop(0, per_kv // stack, heads_step, 0)

    chunk = 16

    def norm_step(i, carry):
        r = pl.ds(pl.multiple_of(i * chunk, chunk), chunk)
        stream = (res_ref[r, :].astype(jnp.float32) + attended[r, :].astype(jnp.float32)).astype(
            jnp.bfloat16
        )
        stream_ref[r, :] = stream
        sf = stream.astype(jnp.float32)
        inv = lax.rsqrt(jnp.mean(sf * sf, -1, keepdims=True) + 1e-06)
        normed[r, :] = (sf * inv * gain_ref[...].astype(jnp.float32)).astype(jnp.bfloat16)
        return carry

    lax.fori_loop(0, rows // chunk, norm_step, 0)

    if not placing:
        return
    tile = 512

    def place_step(i, carry):
        c = pl.ds(pl.multiple_of(i * tile, tile), tile)
        rows_ref[:, c] = jnp.dot(
            place_ref[...], normed[:, c], preferred_element_type=jnp.float32
        ).astype(jnp.bfloat16)
        return carry

    lax.fori_loop(0, normed.shape[1] // tile, place_step, 0)


def attention(n, kv_heads, queries, kv, segcol, residual, gain, place=None):
    rows, width = queries.shape
    reach = min(REACH, n - 2)
    vmem = pl.BlockSpec(memory_space=pltpu.VMEM)
    placing = place is not None
    sent = place.shape[0] if placing else rows
    operands = (queries, kv, segcol, residual, gain) + ((place,) if placing else ())
    scratch = [
        pltpu.VMEM((reach + 1,) + kv.shape, jnp.bfloat16),
        pltpu.VMEM((rows, (reach + 1) * rows), jnp.float32),
        pltpu.VMEM((2 * kv_heads, (reach + 1) * rows, HEAD_SIZE), jnp.bfloat16),
        pltpu.VMEM((rows, width), jnp.bfloat16),
    ]
    if placing:
        scratch.append(pltpu.VMEM((rows, width), jnp.bfloat16))
    return pl.pallas_call(
        functools.partial(attention_kernel, n, kv_heads, placing),
        out_shape=(
            jax.ShapeDtypeStruct((rows, width), jnp.bfloat16),
            jax.ShapeDtypeStruct((sent, width), jnp.bfloat16),
        ),
        in_specs=[vmem] * len(operands),
        out_specs=(vmem, vmem),
        scratch_shapes=scratch + [
            pltpu.SemaphoreType.DMA((reach + 1,)),
            pltpu.SemaphoreType.DMA((reach + 1,)),
        ],
        compiler_params=pltpu.CompilerParams(
            collective_id=0, has_side_effects=True, vmem_limit_bytes=40 * 1024 * 1024
        ),
        name="attention",
    )(*operands)


def experts_kernel(
    n, capacity, tokens_ref, stream_ref, codes_ref, hi_ref, lo_ref,
    gate0, up0, down0, gate1, up1, down1,
    out_ref,
    line, codes, x_out, x_in, feed, hidden, result, returned, w_gate, w_up, w_down,
    w_sem, recv_sem, up_sem, down_sem, code_recv, code_up, code_down, x_send, x_recv, back_send, back_recv,
):
    planes = n // 4
    n_experts = n // 2
    last = planes - 1
    me = lax.axis_index("ep")
    z = me // 4
    x = lax.rem(me // 2, 2)
    c = lax.rem(me, 2)
    expert = me // 2
    partner = me + 2 - 4 * x
    partner_expert = expert + 1 - 2 * x
    rows, width = tokens_ref.shape
    ffe = down0.shape[0]

    barrier = pltpu.get_barrier_semaphore()
    for k in range(1, n_experts):
        pl.semaphore_signal(
            barrier, inc=1, device_id={"ep": lax.rem(me + 2 * k, n)}, device_id_type=MESH
        )

    loads = []
    for j, (g, u, d) in enumerate(((gate0, up0, down0), (gate1, up1, down1))):
        part = pl.ds(j * ffe, ffe)
        for k, (src, dst) in enumerate(
            ((g, w_gate.at[:, part]), (u, w_up.at[:, part]), (d, w_down.at[part, :]))
        ):
            load = pltpu.make_async_copy(src, dst, w_sem.at[3 * j + k])
            load.start()
            loads.append(load)

    line[z] = tokens_ref[...]
    codes[z] = codes_ref[...]
    pl.semaphore_wait(barrier, n_experts - 1)

    def hops(b, upward):
        target = {"ep": lax.rem(me + 4, n) if upward else lax.rem(me + n - 4, n)}
        return (
            pltpu.make_async_remote_copy(
                src_ref=codes.at[b], dst_ref=codes.at[b],
                send_sem=(code_up if upward else code_down).at[b], recv_sem=code_recv.at[b],
                device_id=target, device_id_type=MESH,
            ),
            pltpu.make_async_remote_copy(
                src_ref=line.at[b], dst_ref=line.at[b],
                send_sem=(up_sem if upward else down_sem).at[b], recv_sem=recv_sem.at[b],
                device_id=target, device_id_type=MESH,
            ),
        )

    def swap(b):
        return pltpu.make_async_remote_copy(
            src_ref=x_out.at[b], dst_ref=x_in.at[b],
            send_sem=x_send.at[b], recv_sem=x_recv.at[b],
            device_id={"ep": partner}, device_id_type=MESH,
        )

    def back(b, other):
        side = 1 - x if other else x
        return pltpu.make_async_remote_copy(
            src_ref=result.at[b, pl.ds(capacity * other, capacity)],
            dst_ref=returned.at[pl.ds(pl.multiple_of(expert * capacity, capacity), capacity)],
            send_sem=back_send.at[2 * b + other], recv_sem=back_recv.at[expert],
            device_id={"ep": b * 4 + side * 2 + c}, device_id_type=MESH,
        )

    slots = lax.broadcasted_iota(jnp.int32, (capacity, rows), 0).astype(jnp.float32)
    tile = 512
    tiles = width // tile

    def pack(b, e, put):
        place = (codes[b, e] == slots).astype(jnp.bfloat16)

        def step(i, carry):
            col = pl.ds(pl.multiple_of(i * tile, tile), tile)
            put(col, jnp.dot(
                place, line[b, :, col], preferred_element_type=jnp.float32
            ).astype(jnp.bfloat16))
            return carry

        lax.fori_loop(0, tiles, step, 0)

    def arrive(b):
        @pl.when(b != z)
        def _():
            for copy in hops(b, True):
                copy.wait_recv()

        @pl.when((b <= z) & (z < last))
        def _():
            for copy in hops(b, True):
                copy.start()

        @pl.when((b >= z) & (z > 0))
        def _():
            for copy in hops(b, False):
                copy.start()

        def put(col, value):
            x_out[b, :, col] = value

        pack(b, partner_expert, put)
        swap(b).start()

    def order(i):
        low = jnp.minimum(z, last - z)
        b = jnp.where((low == 1) & (i < 2), 1 - i, i)
        return jnp.where(z < planes // 2, b, last - b)

    def put_feed(col, value):
        feed[0:capacity, col] = value

    hidden_tile = 256

    def step(i, carry):
        b = order(i)
        inner = (z > 0) & (z < last)

        @pl.when((i != 2) | jnp.logical_not(inner))
        def _():
            arrive(b)

        @pl.when((i == 1) & inner)
        def _():
            arrive(order(2))

        pack(b, expert, put_feed)

        @pl.when(i == 0)
        def _():
            for load in loads:
                load.wait()

        swap(b).wait_recv()
        feed[capacity : 2 * capacity, :] = x_in[b]

        def hidden_step(k, inner_carry):
            col = pl.ds(pl.multiple_of(k * hidden_tile, hidden_tile), hidden_tile)
            gate = jnp.dot(feed[...], w_gate[:, col], preferred_element_type=jnp.float32)
            upward = jnp.dot(feed[...], w_up[:, col], preferred_element_type=jnp.float32)
            hidden[:, col] = (jax.nn.silu(gate) * upward).astype(jnp.bfloat16)
            return inner_carry

        lax.fori_loop(0, 2 * ffe // hidden_tile, hidden_step, 0)

        def down_step(k, inner_carry):
            col = pl.ds(pl.multiple_of(k * tile, tile), tile)
            result[b, :, col] = jnp.dot(
                hidden[...], w_down[:, col], preferred_element_type=jnp.float32
            ).astype(jnp.bfloat16)
            return inner_carry

        lax.fori_loop(0, tiles, down_step, 0)

        back(b, 1).start()

        @pl.when(b != z)
        def _():
            back(b, 0).start()

        @pl.when(b == z)
        def _():
            returned[pl.ds(pl.multiple_of(expert * capacity, capacity), capacity), :] = result[
                b, 0:capacity
            ]

        return carry

    lax.fori_loop(0, planes, step, 0)

    for e in range(n_experts):
        @pl.when(expert != e)
        def _():
            pltpu.make_async_remote_copy(
                src_ref=result.at[0, pl.ds(0, capacity)],
                dst_ref=returned.at[pl.ds(e * capacity, capacity)],
                send_sem=back_send.at[0], recv_sem=back_recv.at[e],
                device_id={"ep": partner}, device_id_type=MESH,
            ).wait_recv()

    def mix_step(i, carry):
        col = pl.ds(pl.multiple_of(i * tile, tile), tile)
        picked = returned[:, col]
        mixed = jnp.dot(hi_ref[...], picked, preferred_element_type=jnp.float32)
        mixed += jnp.dot(lo_ref[...], picked, preferred_element_type=jnp.float32)
        out_ref[:, col] = (stream_ref[:, col].astype(jnp.float32) + mixed).astype(jnp.bfloat16)
        return carry

    lax.fori_loop(0, tiles, mix_step, 0)

    for b in range(planes):
        @pl.when((b <= z) & (z < last))
        def _():
            for copy in hops(b, True):
                copy.wait_send()

        @pl.when((b >= z) & (z > 0))
        def _():
            for copy in hops(b, False):
                copy.wait_send()

        swap(b).wait_send()
        back(b, 1).wait_send()

        @pl.when(b != z)
        def _():
            back(b, 0).wait_send()


def run_experts(n, capacity, tokens, stream, codes, mix_hi, mix_lo, weights):
    rows, width = tokens.shape
    ffe = weights[2].shape[0]
    planes = n // 4
    n_experts = n // 2
    vmem = pl.BlockSpec(memory_space=pltpu.VMEM)
    anywhere = pl.BlockSpec(memory_space=pl.ANY)
    half = jnp.bfloat16
    dma = pltpu.SemaphoreType.DMA
    return pl.pallas_call(
        functools.partial(experts_kernel, n, capacity),
        out_shape=jax.ShapeDtypeStruct((rows, width), half),
        in_specs=[vmem] * 5 + [anywhere] * 6,
        out_specs=vmem,
        scratch_shapes=[
            pltpu.VMEM((planes, rows, width), half),
            pltpu.VMEM((planes, n_experts, 1, rows), jnp.float32),
            pltpu.VMEM((planes, capacity, width), half),
            pltpu.VMEM((planes, capacity, width), half),
            pltpu.VMEM((2 * capacity, width), half),
            pltpu.VMEM((2 * capacity, 2 * ffe), half),
            pltpu.VMEM((planes, 2 * capacity, width), half),
            pltpu.VMEM((n_experts * capacity, width), half),
            pltpu.VMEM((width, 2 * ffe), half),
            pltpu.VMEM((width, 2 * ffe), half),
            pltpu.VMEM((2 * ffe, width), half),
            dma((6,)), dma((planes,)), dma((planes,)), dma((planes,)),
            dma((planes,)), dma((planes,)), dma((planes,)),
            dma((planes,)), dma((planes,)), dma((2 * planes,)), dma((n_experts,)),
        ],
        compiler_params=pltpu.CompilerParams(
            collective_id=1, has_side_effects=True, vmem_limit_bytes=56 * 1024 * 1024
        ),
        name="experts",
    )(tokens, stream, codes, mix_hi, mix_lo, *weights)


def local(
    queries, keys, values, segment_ids, residual, norm_gain, route_ids, route_weights,
    w_gate, w_up, w_down,
):
    rows, width = residual.shape
    n = lax.axis_size("ep")
    kv_heads = keys.shape[1] // HEAD_SIZE
    n_experts = n // 2
    topk = route_ids.shape[1]
    capacity = max(2, 2 * rows * topk // n_experts)

    swap = [(i, i ^ 1) for i in range(n)]
    other_gate = lax.ppermute(w_gate[0], "ep", swap)
    other_up = lax.ppermute(w_up[0], "ep", swap)
    other_down = lax.ppermute(w_down[0], "ep", swap)

    seg_row = jnp.zeros((SEG_ROWS, 2 * keys.shape[1]), jnp.bfloat16)
    seg_row = lax.dynamic_update_slice(
        seg_row, jnp.broadcast_to(segment_ids.astype(jnp.bfloat16)[None, :], (SEG_ROWS, rows)), (0, 0)
    )
    kv = jnp.concatenate([jnp.concatenate([keys, values], 1), seg_row], 0)
    segcol = segment_ids.astype(jnp.float32)[:, None]

    experts = jnp.arange(n_experts, dtype=jnp.int32)
    hit = route_ids[:, :, None] == experts[None, None, :]
    named = jnp.any(hit, 1)
    weight = jnp.sum(jnp.where(hit, route_weights[:, :, None], 0.0), 1)
    below = jnp.tril(jnp.ones((rows, rows), jnp.bfloat16), -1)
    slot = jnp.dot(below, named.astype(jnp.bfloat16), preferred_element_type=jnp.float32).astype(jnp.int32)
    code = jnp.where(named, slot, -1)
    slots = jnp.arange(capacity, dtype=jnp.int32)
    place = (code.T[:, None, :] == slots[None, :, None]).astype(jnp.bfloat16)
    place = place.reshape(n_experts * capacity, rows)
    mix = jnp.where(code[:, :, None] == slots[None, None, :], weight[:, :, None], 0.0)
    mix = mix.reshape(rows, n_experts * capacity)
    mix_hi = mix.astype(jnp.bfloat16)
    mix_lo = (mix - mix_hi.astype(jnp.float32)).astype(jnp.bfloat16)

    if n == 16:
        codes = code.T.astype(jnp.float32).reshape(n_experts, 1, rows)
        stream, normed = attention(n, kv_heads, queries, kv, segcol, residual, norm_gain[None, :])
        weights = (w_gate[0], w_up[0], w_down[0], other_gate, other_up, other_down)
        return run_experts(n, capacity, normed, stream, codes, mix_hi, mix_lo, weights)

    stream, outgoing = attention(n, kv_heads, queries, kv, segcol, residual, norm_gain[None, :], place)

    groups = [[c for c in range(k, n, 2)] for k in range(2)]
    arrived = lax.all_to_all(
        outgoing.reshape(n_experts, capacity, width), "ep", split_axis=0, concat_axis=0,
        axis_index_groups=groups, tiled=True,
    ).reshape(-1, width)

    def half(gate_half, up_half, down_half):
        gate = jnp.dot(arrived, gate_half, preferred_element_type=jnp.float32)
        upward = jnp.dot(arrived, up_half, preferred_element_type=jnp.float32)
        hidden = (jax.nn.silu(gate) * upward).astype(jnp.bfloat16)
        return jnp.dot(hidden, down_half, preferred_element_type=jnp.float32)

    out = half(w_gate[0], w_up[0], w_down[0]) + half(other_gate, other_up, other_down)
    returned = lax.all_to_all(
        out.astype(jnp.bfloat16).reshape(n_experts, capacity, width), "ep", split_axis=0,
        concat_axis=0, axis_index_groups=groups, tiled=True,
    ).reshape(-1, width)
    mixed = jnp.dot(mix_hi, returned, preferred_element_type=jnp.float32) + jnp.dot(
        mix_lo, returned, preferred_element_type=jnp.float32
    )
    return (stream.astype(jnp.float32) + mixed).astype(jnp.bfloat16)


def solution(mesh):
    tokens = P(("group", "ep"), None)
    split = P("ep", None, None)
    placed = (
        tokens, tokens, tokens, P(("group", "ep")), tokens, P(), tokens, tokens, split, split, split,
    )
    return jax.shard_map(local, mesh=mesh, in_specs=placed, out_specs=tokens, check_vma=False)
```

```python
import functools
import math

import jax
import jax.numpy as jnp
from jax import lax
from jax.experimental import pallas as pl
from jax.experimental.pallas import tpu as pltpu
from jax.sharding import PartitionSpec as P

HEAD_SIZE = 128
REACH = 8
NEGATIVE = -1e30
MESH = pl.DeviceIdType.MESH
SEG_ROWS = 16


def nt_dot(a, b):
    return lax.dot_general(a, b, (((1,), (1,)), ((), ())), preferred_element_type=jnp.float32)


def attention_kernel(
    n, kv_heads, placing, q_ref, kv_ref, segcol_ref, res_ref, gain_ref, *rest
):
    if placing:
        place_ref, stream_ref, rows_ref, held, bias, all_kv, attended, normed, send_sem, recv_sem = rest
    else:
        stream_ref, normed, held, bias, all_kv, attended, send_sem, recv_sem = rest
    me = lax.axis_index("ep")
    rows = q_ref.shape[0]
    heads = q_ref.shape[1] // HEAD_SIZE
    per_kv = heads // kv_heads
    reach = min(REACH, n - 2)

    core = lax.rem(me, 2)
    sibling = me + 1 - 2 * core
    steps = range(2, reach + 1, 2)

    barrier = pltpu.get_barrier_semaphore()
    for d in steps:
        pl.semaphore_signal(
            barrier, inc=1, device_id={"ep": lax.rem(me + n - d, n)}, device_id_type=MESH
        )
    pl.semaphore_signal(barrier, inc=1, device_id={"ep": sibling}, device_id_type=MESH)
    pl.semaphore_wait(barrier, len(steps) + 1)

    def direct(d):
        return pltpu.make_async_remote_copy(
            src_ref=kv_ref, dst_ref=held.at[d],
            send_sem=send_sem.at[d], recv_sem=recv_sem.at[d],
            device_id={"ep": lax.rem(me + d, n)}, device_id_type=MESH,
        )

    def passed_on(k):
        return pltpu.make_async_remote_copy(
            src_ref=held.at[2 * k + 2 * core], dst_ref=held.at[2 * k + 1],
            send_sem=send_sem.at[2 * k + 1], recv_sem=recv_sem.at[2 * k + 1],
            device_id={"ep": sibling}, device_id_type=MESH,
        )

    for d in steps:
        direct(d).start()
    held[0] = kv_ref[...]
    for k in range(reach // 2):
        if k == 0:
            @pl.when(core == 1)
            def _():
                direct(2).wait_recv()
        else:
            direct(2 * k + 2 * core).wait_recv()
        passed_on(k).start()

    @pl.when(core == 0)
    def _():
        direct(reach).wait_recv()

    for k in range(reach // 2):
        passed_on(k).wait()
    for d in steps:
        direct(d).wait_send()

    query_seg = segcol_ref[...]
    t = lax.broadcasted_iota(jnp.int32, (rows, rows), 0)
    u = lax.broadcasted_iota(jnp.int32, (rows, rows), 1)
    for d in range(reach + 1):
        key_seg = held[d, rows : rows + SEG_ROWS, 0:rows][0:1].astype(jnp.float32)
        allowed = (key_seg == query_seg) & (u - d * rows <= t) & (u + (me - d) * rows >= 0)
        bias[:, d * rows : (d + 1) * rows] = jnp.where(allowed, 0.0, NEGATIVE)
        for part in range(2 * kv_heads):
            all_kv[part, d * rows : (d + 1) * rows, :] = held[
                d, 0:rows, part * HEAD_SIZE : (part + 1) * HEAD_SIZE
            ]

    scale = math.log2(math.e) / math.sqrt(HEAD_SIZE)

    stack = 4

    def some_heads(h, g):
        cols = [
            pl.ds(pl.multiple_of((h + j) * HEAD_SIZE, HEAD_SIZE), HEAD_SIZE) for j in range(stack)
        ]
        q = jnp.concatenate([q_ref[:, col] for col in cols], 0)
        s = nt_dot(q, all_kv[g]) * scale
        s = (s.reshape(stack, rows, s.shape[1]) + bias[...][None]).reshape(s.shape)
        top = jnp.max(s, -1, keepdims=True)
        p = jnp.exp2(s - top)
        total = jnp.sum(p, -1, keepdims=True)
        pv = jnp.dot(
            p.astype(jnp.bfloat16), all_kv[kv_heads + g], preferred_element_type=jnp.float32
        )
        done = (pv / total).astype(jnp.bfloat16)
        for j, col in enumerate(cols):
            attended[:, col] = done[j * rows : (j + 1) * rows]

    def heads_step(i, carry):
        for g in range(kv_heads):
            some_heads(i * stack + g * per_kv, g)
        return carry

    lax.fori_loop(0, per_kv // stack, heads_step, 0)

    chunk = 16

    def norm_step(i, carry):
        r = pl.ds(pl.multiple_of(i * chunk, chunk), chunk)
        stream = (res_ref[r, :].astype(jnp.float32) + attended[r, :].astype(jnp.float32)).astype(
            jnp.bfloat16
        )
        stream_ref[r, :] = stream
        sf = stream.astype(jnp.float32)
        inv = lax.rsqrt(jnp.mean(sf * sf, -1, keepdims=True) + 1e-06)
        normed[r, :] = (sf * inv * gain_ref[...].astype(jnp.float32)).astype(jnp.bfloat16)
        return carry

    lax.fori_loop(0, rows // chunk, norm_step, 0)

    if not placing:
        return
    tile = 512

    def place_step(i, carry):
        c = pl.ds(pl.multiple_of(i * tile, tile), tile)
        rows_ref[:, c] = jnp.dot(
            place_ref[...], normed[:, c], preferred_element_type=jnp.float32
        ).astype(jnp.bfloat16)
        return carry

    lax.fori_loop(0, normed.shape[1] // tile, place_step, 0)


def attention(n, kv_heads, queries, kv, segcol, residual, gain, place=None):
    rows, width = queries.shape
    reach = min(REACH, n - 2)
    vmem = pl.BlockSpec(memory_space=pltpu.VMEM)
    placing = place is not None
    sent = place.shape[0] if placing else rows
    operands = (queries, kv, segcol, residual, gain) + ((place,) if placing else ())
    scratch = [
        pltpu.VMEM((reach + 1,) + kv.shape, jnp.bfloat16),
        pltpu.VMEM((rows, (reach + 1) * rows), jnp.float32),
        pltpu.VMEM((2 * kv_heads, (reach + 1) * rows, HEAD_SIZE), jnp.bfloat16),
        pltpu.VMEM((rows, width), jnp.bfloat16),
    ]
    if placing:
        scratch.append(pltpu.VMEM((rows, width), jnp.bfloat16))
    return pl.pallas_call(
        functools.partial(attention_kernel, n, kv_heads, placing),
        out_shape=(
            jax.ShapeDtypeStruct((rows, width), jnp.bfloat16),
            jax.ShapeDtypeStruct((sent, width), jnp.bfloat16),
        ),
        in_specs=[vmem] * len(operands),
        out_specs=(vmem, vmem),
        scratch_shapes=scratch + [
            pltpu.SemaphoreType.DMA((reach + 1,)),
            pltpu.SemaphoreType.DMA((reach + 1,)),
        ],
        compiler_params=pltpu.CompilerParams(
            collective_id=0, has_side_effects=True, vmem_limit_bytes=40 * 1024 * 1024
        ),
        name="attention",
    )(*operands)


def experts_kernel(
    n, capacity, tokens_ref, stream_ref, codes_ref, hi_ref, lo_ref,
    gate0, up0, down0, gate1, up1, down1,
    out_ref,
    line, codes, x_out, x_in, feed, hidden, result, returned, w_gate, w_up, w_down,
    w_sem, recv_sem, up_sem, down_sem, code_recv, code_up, code_down, x_send, x_recv, back_send, back_recv,
):
    planes = n // 4
    n_experts = n // 2
    last = planes - 1
    me = lax.axis_index("ep")
    z = me // 4
    x = lax.rem(me // 2, 2)
    c = lax.rem(me, 2)
    expert = me // 2
    partner = me + 2 - 4 * x
    partner_expert = expert + 1 - 2 * x
    rows, width = tokens_ref.shape
    ffe = down0.shape[0]

    barrier = pltpu.get_barrier_semaphore()
    for k in range(1, n_experts):
        pl.semaphore_signal(
            barrier, inc=1, device_id={"ep": lax.rem(me + 2 * k, n)}, device_id_type=MESH
        )

    loads = []
    for j, (g, u, d) in enumerate(((gate0, up0, down0), (gate1, up1, down1))):
        part = pl.ds(j * ffe, ffe)
        for k, (src, dst) in enumerate(
            ((g, w_gate.at[:, part]), (u, w_up.at[:, part]), (d, w_down.at[part, :]))
        ):
            load = pltpu.make_async_copy(src, dst, w_sem.at[3 * j + k])
            load.start()
            loads.append(load)

    line[z] = tokens_ref[...]
    codes[z] = codes_ref[...]
    pl.semaphore_wait(barrier, n_experts - 1)

    def hops(b, upward):
        target = {"ep": lax.rem(me + 4, n) if upward else lax.rem(me + n - 4, n)}
        return (
            pltpu.make_async_remote_copy(
                src_ref=codes.at[b], dst_ref=codes.at[b],
                send_sem=(code_up if upward else code_down).at[b], recv_sem=code_recv.at[b],
                device_id=target, device_id_type=MESH,
            ),
            pltpu.make_async_remote_copy(
                src_ref=line.at[b], dst_ref=line.at[b],
                send_sem=(up_sem if upward else down_sem).at[b], recv_sem=recv_sem.at[b],
                device_id=target, device_id_type=MESH,
            ),
        )

    def swap(b):
        return pltpu.make_async_remote_copy(
            src_ref=x_out.at[b], dst_ref=x_in.at[b],
            send_sem=x_send.at[b], recv_sem=x_recv.at[b],
            device_id={"ep": partner}, device_id_type=MESH,
        )

    def back(b, other):
        side = 1 - x if other else x
        return pltpu.make_async_remote_copy(
            src_ref=result.at[b, pl.ds(capacity * other, capacity)],
            dst_ref=returned.at[pl.ds(pl.multiple_of(expert * capacity, capacity), capacity)],
            send_sem=back_send.at[2 * b + other], recv_sem=back_recv.at[expert],
            device_id={"ep": b * 4 + side * 2 + c}, device_id_type=MESH,
        )

    slots = lax.broadcasted_iota(jnp.int32, (capacity, rows), 0).astype(jnp.float32)
    tile = 512
    tiles = width // tile

    def pack(b, e, put):
        place = (codes[b, e] == slots).astype(jnp.bfloat16)

        def step(i, carry):
            col = pl.ds(pl.multiple_of(i * tile, tile), tile)
            put(col, jnp.dot(
                place, line[b, :, col], preferred_element_type=jnp.float32
            ).astype(jnp.bfloat16))
            return carry

        lax.fori_loop(0, tiles, step, 0)

    def arrive(b):
        @pl.when(b != z)
        def _():
            for copy in hops(b, True):
                copy.wait_recv()

        @pl.when((b <= z) & (z < last))
        def _():
            for copy in hops(b, True):
                copy.start()

        @pl.when((b >= z) & (z > 0))
        def _():
            for copy in hops(b, False):
                copy.start()

        def put(col, value):
            x_out[b, :, col] = value

        pack(b, partner_expert, put)
        swap(b).start()

    def order(i):
        low = jnp.minimum(z, last - z)
        b = jnp.where((low == 1) & (i < 2), 1 - i, i)
        return jnp.where(z < planes // 2, b, last - b)

    def put_feed(col, value):
        feed[0:capacity, col] = value

    hidden_tile = 256

    def step(i, carry):
        b = order(i)
        inner = (z > 0) & (z < last)

        @pl.when((i != 2) | jnp.logical_not(inner))
        def _():
            arrive(b)

        @pl.when((i == 1) & inner)
        def _():
            arrive(order(2))

        pack(b, expert, put_feed)

        @pl.when(i == 0)
        def _():
            for load in loads:
                load.wait()

        swap(b).wait_recv()
        feed[capacity : 2 * capacity, :] = x_in[b]

        def hidden_step(k, inner_carry):
            col = pl.ds(pl.multiple_of(k * hidden_tile, hidden_tile), hidden_tile)
            gate = jnp.dot(feed[...], w_gate[:, col], preferred_element_type=jnp.float32)
            upward = jnp.dot(feed[...], w_up[:, col], preferred_element_type=jnp.float32)
            hidden[:, col] = (jax.nn.silu(gate) * upward).astype(jnp.bfloat16)
            return inner_carry

        lax.fori_loop(0, 2 * ffe // hidden_tile, hidden_step, 0)

        def down_step(k, inner_carry):
            col = pl.ds(pl.multiple_of(k * tile, tile), tile)
            result[b, :, col] = jnp.dot(
                hidden[...], w_down[:, col], preferred_element_type=jnp.float32
            ).astype(jnp.bfloat16)
            return inner_carry

        lax.fori_loop(0, tiles, down_step, 0)

        back(b, 1).start()

        @pl.when(b != z)
        def _():
            back(b, 0).start()

        @pl.when(b == z)
        def _():
            returned[pl.ds(pl.multiple_of(expert * capacity, capacity), capacity), :] = result[
                b, 0:capacity
            ]

        return carry

    lax.fori_loop(0, planes, step, 0)

    for e in range(n_experts):
        @pl.when(expert != e)
        def _():
            pltpu.make_async_remote_copy(
                src_ref=result.at[0, pl.ds(0, capacity)],
                dst_ref=returned.at[pl.ds(e * capacity, capacity)],
                send_sem=back_send.at[0], recv_sem=back_recv.at[e],
                device_id={"ep": partner}, device_id_type=MESH,
            ).wait_recv()

    def mix_step(i, carry):
        col = pl.ds(pl.multiple_of(i * tile, tile), tile)
        picked = returned[:, col]
        mixed = jnp.dot(hi_ref[...], picked, preferred_element_type=jnp.float32)
        mixed += jnp.dot(lo_ref[...], picked, preferred_element_type=jnp.float32)
        out_ref[:, col] = (stream_ref[:, col].astype(jnp.float32) + mixed).astype(jnp.bfloat16)
        return carry

    lax.fori_loop(0, tiles, mix_step, 0)

    for b in range(planes):
        @pl.when((b <= z) & (z < last))
        def _():
            for copy in hops(b, True):
                copy.wait_send()

        @pl.when((b >= z) & (z > 0))
        def _():
            for copy in hops(b, False):
                copy.wait_send()

        swap(b).wait_send()
        back(b, 1).wait_send()

        @pl.when(b != z)
        def _():
            back(b, 0).wait_send()


def run_experts(n, capacity, tokens, stream, codes, mix_hi, mix_lo, weights):
    rows, width = tokens.shape
    ffe = weights[2].shape[0]
    planes = n // 4
    n_experts = n // 2
    vmem = pl.BlockSpec(memory_space=pltpu.VMEM)
    anywhere = pl.BlockSpec(memory_space=pl.ANY)
    half = jnp.bfloat16
    dma = pltpu.SemaphoreType.DMA
    return pl.pallas_call(
        functools.partial(experts_kernel, n, capacity),
        out_shape=jax.ShapeDtypeStruct((rows, width), half),
        in_specs=[vmem] * 5 + [anywhere] * 6,
        out_specs=vmem,
        scratch_shapes=[
            pltpu.VMEM((planes, rows, width), half),
            pltpu.VMEM((planes, n_experts, 1, rows), jnp.float32),
            pltpu.VMEM((planes, capacity, width), half),
            pltpu.VMEM((planes, capacity, width), half),
            pltpu.VMEM((2 * capacity, width), half),
            pltpu.VMEM((2 * capacity, 2 * ffe), half),
            pltpu.VMEM((planes, 2 * capacity, width), half),
            pltpu.VMEM((n_experts * capacity, width), half),
            pltpu.VMEM((width, 2 * ffe), half),
            pltpu.VMEM((width, 2 * ffe), half),
            pltpu.VMEM((2 * ffe, width), half),
            dma((6,)), dma((planes,)), dma((planes,)), dma((planes,)),
            dma((planes,)), dma((planes,)), dma((planes,)),
            dma((planes,)), dma((planes,)), dma((2 * planes,)), dma((n_experts,)),
        ],
        compiler_params=pltpu.CompilerParams(
            collective_id=1, has_side_effects=True, vmem_limit_bytes=56 * 1024 * 1024
        ),
        name="experts",
    )(tokens, stream, codes, mix_hi, mix_lo, *weights)


def local(
    queries, keys, values, segment_ids, residual, norm_gain, route_ids, route_weights,
    w_gate, w_up, w_down,
):
    rows, width = residual.shape
    n = lax.axis_size("ep")
    kv_heads = keys.shape[1] // HEAD_SIZE
    n_experts = n // 2
    topk = route_ids.shape[1]
    capacity = max(2, 2 * rows * topk // n_experts)

    swap = [(i, i ^ 1) for i in range(n)]
    other_gate = lax.ppermute(w_gate[0], "ep", swap)
    other_up = lax.ppermute(w_up[0], "ep", swap)
    other_down = lax.ppermute(w_down[0], "ep", swap)

    seg_row = jnp.zeros((SEG_ROWS, 2 * keys.shape[1]), jnp.bfloat16)
    seg_row = lax.dynamic_update_slice(
        seg_row, jnp.broadcast_to(segment_ids.astype(jnp.bfloat16)[None, :], (SEG_ROWS, rows)), (0, 0)
    )
    kv = jnp.concatenate([jnp.concatenate([keys, values], 1), seg_row], 0)
    segcol = segment_ids.astype(jnp.float32)[:, None]

    experts = jnp.arange(n_experts, dtype=jnp.int32)
    hit = route_ids[:, :, None] == experts[None, None, :]
    named = jnp.any(hit, 1)
    weight = jnp.sum(jnp.where(hit, route_weights[:, :, None], 0.0), 1)
    below = jnp.tril(jnp.ones((rows, rows), jnp.bfloat16), -1)
    slot = jnp.dot(below, named.astype(jnp.bfloat16), preferred_element_type=jnp.float32).astype(jnp.int32)
    code = jnp.where(named, slot, -1)
    slots = jnp.arange(capacity, dtype=jnp.int32)
    place = (code.T[:, None, :] == slots[None, :, None]).astype(jnp.bfloat16)
    place = place.reshape(n_experts * capacity, rows)
    mix = jnp.where(code[:, :, None] == slots[None, None, :], weight[:, :, None], 0.0)
    mix = mix.reshape(rows, n_experts * capacity)
    mix_hi = mix.astype(jnp.bfloat16)
    mix_lo = (mix - mix_hi.astype(jnp.float32)).astype(jnp.bfloat16)

    if n == 16:
        codes = code.T.astype(jnp.float32).reshape(n_experts, 1, rows)
        stream, normed = attention(n, kv_heads, queries, kv, segcol, residual, norm_gain[None, :])
        weights = (w_gate[0], w_up[0], w_down[0], other_gate, other_up, other_down)
        return run_experts(n, capacity, normed, stream, codes, mix_hi, mix_lo, weights)

    stream, outgoing = attention(n, kv_heads, queries, kv, segcol, residual, norm_gain[None, :], place)

    groups = [[c for c in range(k, n, 2)] for k in range(2)]
    arrived = lax.all_to_all(
        outgoing.reshape(n_experts, capacity, width), "ep", split_axis=0, concat_axis=0,
        axis_index_groups=groups, tiled=True,
    ).reshape(-1, width)

    def half(gate_half, up_half, down_half):
        gate = jnp.dot(arrived, gate_half, preferred_element_type=jnp.float32)
        upward = jnp.dot(arrived, up_half, preferred_element_type=jnp.float32)
        hidden = (jax.nn.silu(gate) * upward).astype(jnp.bfloat16)
        return jnp.dot(hidden, down_half, preferred_element_type=jnp.float32)

    out = half(w_gate[0], w_up[0], w_down[0]) + half(other_gate, other_up, other_down)
    returned = lax.all_to_all(
        out.astype(jnp.bfloat16).reshape(n_experts, capacity, width), "ep", split_axis=0,
        concat_axis=0, axis_index_groups=groups, tiled=True,
    ).reshape(-1, width)
    mixed = jnp.dot(mix_hi, returned, preferred_element_type=jnp.float32) + jnp.dot(
        mix_lo, returned, preferred_element_type=jnp.float32
    )
    return (stream.astype(jnp.float32) + mixed).astype(jnp.bfloat16)


def solution(mesh):
    tokens = P(("group", "ep"), None)
    split = P("ep", None, None)
    placed = (
        tokens, tokens, tokens, P(("group", "ep")), tokens, P(), tokens, tokens, split, split, split,
    )
    return jax.shard_map(local, mesh=mesh, in_specs=placed, out_specs=tokens, check_vma=False)
```
